128 devices in a mesh: seq: 16 (over x, y), head: 8 (over z, core).
Axes of the slice: x: 4, y: 4, z: 4, core: 2. Of those that a mesh axis runs over, the one named last changes fastest.
Arguments:
- teacher_queries: bfloat16 [4096, 8192], P('seq', 'head'), may hold values from -5 to 5
- rotated_teacher_keys: bfloat16 [4096, 1024], P('seq', 'head'), may hold values from -5 to 5
- teacher_value_rows: bfloat16 [4096, 1024], P('seq', 'head'), may hold values from -6 to 6
- doc_lengths: int32 [8], replicated, may hold values from 1 to 3072, 4096 in all
- out_proj: bfloat16 [8192, 8192], P('head'), may hold values from -0.0625 to 0.0625
- query_map: float32 [64, 128, 128], P('head'), may hold values from -0.5 to 0.5
- key_map: float32 [64, 128, 128], P('head'), may hold values from -0.5 to 0.5
- beta_weight: float32 [64, 128], P('head'), may hold values from -0.5 to 0.5
- beta_bias: float32 [64], P('head'), may hold values from -5 to 2
Outputs:
- match_loss: float32 [], replicated
- grad_query_map: float32 [64, 128, 128], P('head')
- grad_key_map: float32 [64, 128, 128], P('head')
- grad_beta_weight: float32 [64, 128], P('head')
The draws below stay inside these ranges and needn't reach their ends.
Inputs may be any that keep to these rules, and one draw needn't show every extreme that they name: `doc_lengths`: the documents lie end to end, in order, and fill the 4096 positions; the longest holds three quarters of them.
All inputs are finite; a program needn't handle non-finite values.
Results may differ from the reference program's by a relative error of at most 0.009.
Values may be sent and summed in bfloat16 or wider, within the bound.
A program may use at most 256 MiB of HBM per device.

```python
import math
import jax
import jax.numpy as jnp
import numpy as np
from jax import lax

D = 8192
QUERY_HEADS = 64
KEY_VALUE_HEADS = 8
HEAD_SIZE = 128
SPAN = 64
NDOCS = 8
TOK_DEV = 256
PACKED_TOKENS = 4096
N_HEAD = 8


def draw_teacher_queries(key, part):
    key = jax.random.fold_in(key, 11)
    value_entries = jax.random.normal(key, (PACKED_TOKENS, QUERY_HEADS * HEAD_SIZE), jnp.float32)
    return jnp.clip(value_entries, -5.0, 5.0).astype(jnp.bfloat16)


def draw_rotated_teacher_keys(key, part):
    key = jax.random.fold_in(key, 23)
    value_entries = jax.random.normal(key, (PACKED_TOKENS, KEY_VALUE_HEADS * HEAD_SIZE), jnp.float32)
    return jnp.clip(value_entries, -5.0, 5.0).astype(jnp.bfloat16)


def draw_teacher_value_rows(key, part):
    key = jax.random.fold_in(key, 37)
    phase = (jnp.arange(PACKED_TOKENS) % TOK_DEV).astype(jnp.float32) / TOK_DEV
    whole_phase = jnp.arange(PACKED_TOKENS).astype(jnp.float32) / PACKED_TOKENS
    base_values = jax.random.normal(key, (PACKED_TOKENS, KEY_VALUE_HEADS * HEAD_SIZE), jnp.float32)
    ramp = (0.5 + 1.5 * phase) * (0.6 + 1.4 * whole_phase)
    return jnp.clip(base_values * ramp[:, None], -6.0, 6.0).astype(jnp.bfloat16)


def levels(own_key, dims, shards, smallest, largest):
    level, own = 1.0, jax.random.fold_in(own_key, 6)
    for axis_at, blocks in shards:
        heights = jnp.exp(jax.random.uniform(jax.random.fold_in(own, axis_at), (blocks,), jnp.float32, smallest / len(shards), largest / len(shards)))
        level = level * jnp.repeat(heights, dims[axis_at] // blocks).reshape([-1 if axis == axis_at else 1 for axis in range(len(dims))])
    return level


def split_up(count, total, reach, lean):
    weights = [(1 << 20) // math.isqrt(grade ** lean) + 1 for grade in range(2, count + 1)]
    surplus, holding = total - reach - (count - 1), [1] * (count - 1)
    while surplus > 0:
        movable = [i for i in range(count - 1) if holding[i] < reach]
        pool, remaining = sum([weights[i] for i in movable]), surplus
        for i in movable:
            more = min(reach - holding[i], max(1, remaining * weights[i] // pool), surplus)
            holding[i] = holding[i] + more
            surplus = surplus - more
    return np.array([reach] + holding)


def uneven_parts(rng, amount, total, limit, lean):
    if amount == 2:
        one = jax.random.randint(rng, (), max(1, total - limit), min(limit, total - 1) + 1)
        return jnp.stack([one, total - one])
    tallies = jnp.asarray(split_up(amount, total, limit, lean), jnp.int32)
    twos = (amount - 1) // 2
    donor, sink = tallies[1:1 + 2 * twos:2], tallies[2:2 + 2 * twos:2]
    margin = jnp.minimum(donor - 1, limit - sink)
    shifted = jax.random.randint(jax.random.fold_in(rng, 1), (twos,), 0, 1 << 20) % (margin + 1)
    tallies = tallies.at[1:1 + 2 * twos:2].set(donor - shifted).at[2:2 + 2 * twos:2].set(sink + shifted)
    return tallies[jax.random.permutation(jax.random.fold_in(rng, 2), amount)]


def noise(own_key, shape, spread, reach, cuts=(), kind=jnp.bfloat16):
    values = jax.random.normal(own_key, shape, jnp.float32) * spread
    if len(cuts) > 0:
        values = levels(own_key, shape, cuts, -0.22, 0.18) * values
    return jnp.clip(values, min=-reach, max=reach).astype(kind)


def setup_inputs(seed: int = 0) -> dict:
    keys = jax.random.split(jax.random.key(seed), 10)
    teacher_queries = draw_teacher_queries(jax.random.fold_in(keys[9], 71), 0)
    rotated_teacher_keys = draw_rotated_teacher_keys(jax.random.fold_in(keys[9], 71), 0)
    teacher_value_rows = draw_teacher_value_rows(jax.random.fold_in(keys[9], 71), 0)
    doc_lengths = uneven_parts(keys[3], NDOCS, PACKED_TOKENS, PACKED_TOKENS * 3 // 4, 2).astype(jnp.int32)
    out_proj = noise(keys[4], (QUERY_HEADS * HEAD_SIZE, D), (QUERY_HEADS * HEAD_SIZE) ** -0.5, 0.0625, ((0, 8),))
    query_map = noise(keys[5], (QUERY_HEADS, HEAD_SIZE, HEAD_SIZE), HEAD_SIZE ** -0.5, 0.5, ((0, 8),), jnp.float32)
    key_map = noise(keys[6], (QUERY_HEADS, HEAD_SIZE, HEAD_SIZE), HEAD_SIZE ** -0.5, 0.5, ((0, 8),), jnp.float32)
    beta_weight = noise(keys[7], (QUERY_HEADS, HEAD_SIZE), HEAD_SIZE ** -0.5, 0.5, ((0, 8),), jnp.float32)
    beta_bias = jnp.clip(-5.0 + 7.0 * jax.random.uniform(keys[8], (QUERY_HEADS,), jnp.float32) ** levels(keys[8], (QUERY_HEADS,), ((0, 8),), -0.2, 0.2), -5.0, 2.0)
    return dict(teacher_queries=teacher_queries, rotated_teacher_keys=rotated_teacher_keys, teacher_value_rows=teacher_value_rows, doc_lengths=doc_lengths, out_proj=out_proj, query_map=query_map, key_map=key_map, beta_weight=beta_weight, beta_bias=beta_bias)


highest = lax.Precision.HIGHEST

def doc_index(positions, doc_lengths):
    starts = jnp.cumsum(doc_lengths) - doc_lengths
    inside = (positions[:, None] >= starts[None, 1:]).astype(jnp.int32)
    found_index = lax.optimization_barrier(jnp.sum(inside, axis=1)).astype(jnp.int32)
    return jnp.where(positions < 0, -1, found_index).astype(jnp.int32)

def unit_rows(tensor):
    activated = jax.nn.silu(tensor)
    return activated / jnp.sqrt(lax.optimization_barrier(jnp.sum(activated * activated, axis=-1, keepdims=True)) + 1e-06)

def features(query_rows, teacher_key_rows, query_map, key_map, beta_weight, beta_bias):
    query_units = unit_rows(jnp.einsum('thd,hde->hte', query_rows, query_map, precision=highest))
    key_units = unit_rows(jnp.einsum('thd,hde->hte', teacher_key_rows, key_map, precision=highest))
    logits = jnp.einsum('thd,hd->ht', query_rows, beta_weight, precision=highest) + beta_bias[:, None]
    return (query_units, key_units, jax.nn.sigmoid(logits))

def span_factors(query_units, key_units, strengths, student_value_rows, same_doc, causal):
    block_length = key_units.shape[-2]
    key_width = key_units.shape[-1]
    identity_block = jnp.eye(block_length, dtype=jnp.float32)
    key_gram = jnp.einsum('...id,...jd->...ij', key_units, key_units, precision=highest)
    coupling = strengths[..., :, None] * key_gram * same_doc * (causal - identity_block)
    system = identity_block + coupling
    right_side = strengths[..., None] * jnp.concatenate([key_units, student_value_rows], axis=-1)
    solved = lax.linalg.triangular_solve(system, right_side, left_side=True, lower=True, unit_diagonal=True)
    scores = jnp.einsum('...id,...jd->...ij', query_units, key_units, precision=highest) * same_doc * causal
    return (solved[..., :key_width], solved[..., key_width:], scores)

def span_outputs(query_units, wy_keys, wy_values, scores, starts, lead_flag):
    carried = jnp.einsum('...id,...ed->...ie', query_units, starts, precision=highest)
    removed = jnp.einsum('...jd,...ed->...je', wy_keys, starts, precision=highest)
    carried = carried - jnp.einsum('...ij,...je->...ie', scores, removed, precision=highest)
    fresh_part = jnp.einsum('...ij,...je->...ie', scores, wy_values, precision=highest)
    return lead_flag[..., None] * carried + fresh_part

def teacher_attention(teacher_queries, rotated_teacher_keys, teacher_value_rows, doc_ids):
    query_group_ratio = QUERY_HEADS // KEY_VALUE_HEADS
    positions = jnp.arange(PACKED_TOKENS, dtype=jnp.int32)
    allowed = (positions[None, :] <= positions[:, None]) & (doc_ids[None, :] == doc_ids[:, None])
    score_scale = 1.0 / math.sqrt(HEAD_SIZE)

    def one_head(head_number):
        group_number = (head_number // query_group_ratio).astype(jnp.int32)
        head_query = lax.dynamic_slice_in_dim(teacher_queries, (head_number * HEAD_SIZE).astype(jnp.int32), HEAD_SIZE, 1)
        head_key = lax.dynamic_slice_in_dim(rotated_teacher_keys, (group_number * HEAD_SIZE).astype(jnp.int32), HEAD_SIZE, 1)
        head_value = lax.dynamic_slice_in_dim(teacher_value_rows, (group_number * HEAD_SIZE).astype(jnp.int32), HEAD_SIZE, 1)
        scores = lax.dot_general(head_query.astype(jnp.float32), head_key.astype(jnp.float32), (((1,), (1,)), ((), ())), preferred_element_type=jnp.float32) * score_scale
        masked = jnp.where(allowed, scores, -1e+30)
        row_peak = lax.optimization_barrier(jnp.max(masked, axis=1, keepdims=True))
        weights = jnp.where(allowed, jnp.exp(masked - row_peak), 0.0)
        row_total = lax.optimization_barrier(jnp.sum(weights, axis=1, keepdims=True))
        mixed_sum = jnp.dot(weights.astype(jnp.bfloat16).astype(jnp.float32), head_value.astype(jnp.float32), preferred_element_type=jnp.float32)
        return mixed_sum / row_total
    head_outputs = lax.map(one_head, jnp.arange(QUERY_HEADS, dtype=jnp.int32))
    return jnp.transpose(head_outputs, (1, 0, 2)).reshape(PACKED_TOKENS, QUERY_HEADS * HEAD_SIZE)

def reference(teacher_queries, rotated_teacher_keys, teacher_value_rows, doc_lengths, out_proj, query_map, key_map, beta_weight, beta_bias):
    positions = jnp.arange(PACKED_TOKENS, dtype=jnp.int32)
    doc_ids = doc_index(positions, doc_lengths)
    teacher_out = teacher_attention(teacher_queries, rotated_teacher_keys, teacher_value_rows, doc_ids)
    query_group_ratio = QUERY_HEADS // KEY_VALUE_HEADS
    span_count = PACKED_TOKENS // SPAN
    query_rows = teacher_queries.astype(jnp.float32).reshape(PACKED_TOKENS, QUERY_HEADS, HEAD_SIZE)
    teacher_key_rows = jnp.repeat(rotated_teacher_keys.astype(jnp.float32).reshape(PACKED_TOKENS, KEY_VALUE_HEADS, HEAD_SIZE), query_group_ratio, axis=1)
    student_value_rows = jnp.repeat(teacher_value_rows.astype(jnp.float32).reshape(PACKED_TOKENS, KEY_VALUE_HEADS, HEAD_SIZE), query_group_ratio, axis=1)
    span_docs = doc_ids.reshape(span_count, SPAN)
    before = doc_index(jnp.arange(span_count, dtype=jnp.int32) * SPAN - 1, doc_lengths)
    lead_flag = (span_docs == before[:, None]).astype(jnp.float32)
    tail_flag = (span_docs == span_docs[:, -1:]).astype(jnp.float32)
    same_doc = (span_docs[:, :, None] == span_docs[:, None, :]).astype(jnp.float32)
    causal = jnp.tril(jnp.ones((SPAN, SPAN), jnp.float32))
    identity_matrix = jnp.eye(HEAD_SIZE, dtype=jnp.float32)

    def blocks(tensor):
        shaped = tensor.reshape((tensor.shape[0], span_count, SPAN) + tensor.shape[2:])
        return jnp.moveaxis(shaped, 1, 0)
    value_blocks = blocks(jnp.transpose(student_value_rows, (1, 0, 2)))

    def student(map_for_queries, map_for_keys, weight_for_beta):
        query_units, key_units, strengths = features(query_rows, teacher_key_rows, map_for_queries, map_for_keys, weight_for_beta, beta_bias)

        def advance(state_now, inputs):
            query_block, key_block, strength_block, value_block, same_block, lead_block, tail_block = inputs
            wy_keys, wy_values, scores = span_factors(query_block, key_block, strength_block, value_block, same_block, causal)
            block_out = span_outputs(query_block, wy_keys, wy_values, scores, state_now, lead_block)
            transition = lead_block[-1] * (identity_matrix - jnp.einsum('hid,hie->hde', wy_keys, key_block, precision=highest))
            addition = jnp.einsum('hie,hid->hed', wy_values * tail_block[None, :, None], key_block, precision=highest)
            state_next = jnp.einsum('hed,hdf->hef', state_now, transition, precision=highest) + addition
            return (state_next, block_out)
        start_state = jnp.zeros((QUERY_HEADS, HEAD_SIZE, HEAD_SIZE), jnp.float32)
        final_state, block_outs = lax.scan(jax.checkpoint(advance), start_state, (blocks(query_units), blocks(key_units), blocks(strengths), value_blocks, same_doc, lead_flag, tail_flag))
        per_head = jnp.moveaxis(block_outs, 0, 1).reshape(QUERY_HEADS, PACKED_TOKENS, HEAD_SIZE)
        return jnp.transpose(per_head, (1, 0, 2)).reshape(PACKED_TOKENS, QUERY_HEADS * HEAD_SIZE)
    student_out, backward = jax.vjp(student, query_map, key_map, beta_weight)
    output_gap = (student_out - teacher_out).astype(jnp.bfloat16)
    slice_width = QUERY_HEADS * HEAD_SIZE // N_HEAD
    residual = jnp.zeros((PACKED_TOKENS, D), jnp.float32)
    for group_index in range(N_HEAD):
        group_part = jnp.dot(output_gap[:, group_index * slice_width:(group_index + 1) * slice_width].astype(jnp.float32), out_proj[group_index * slice_width:(group_index + 1) * slice_width].astype(jnp.float32), preferred_element_type=jnp.float32)
        rounded = lax.optimization_barrier(group_part.astype(jnp.bfloat16))
        residual = residual + rounded.astype(jnp.float32)
    match_loss = jnp.sum(residual * residual) / (PACKED_TOKENS * D)
    gap_grad = 2.0 * lax.dot_general(residual.astype(jnp.bfloat16).astype(jnp.float32), out_proj.astype(jnp.float32), (((1,), (1,)), ((), ())), preferred_element_type=jnp.float32)
    grad_query_map, grad_key_map, grad_beta_weight = backward(gap_grad)
    return (match_loss, grad_query_map, grad_key_map, grad_beta_weight)
```

```python
import functools
import math

import jax
import jax.numpy as jnp
from jax import lax
from jax.experimental import pallas as pl
from jax.experimental.pallas import tpu as pltpu
from jax.sharding import PartitionSpec as P

HEAD = 128
ROWS = 256
HEADS = 8
SEQ = 16
NDOCS = 8
WIDTH = 8192
HALF = 512
KEY_BLOCK = 2048
TEAM = 4

f32 = jnp.float32
bf16 = jnp.bfloat16
NN = ((1,), (0,))
NT = ((1,), (1,))
TN = ((0,), (0,))
VMEM_BYTES = 56 * 1024 * 1024
MESH = pl.DeviceIdType.MESH


def mm(a, b, dims):
    return lax.dot_general(a, b, (dims, ((), ())), preferred_element_type=f32)


def split(x):
    hi = x.astype(bf16)
    return hi, (x - hi.astype(f32)).astype(bf16)


def d1(a, b, dims):
    return mm(a.astype(bf16), b.astype(bf16), dims)


def d3(a, b, dims):
    ah, al = split(a)
    bh, bl = split(b)
    return mm(ah, bh, dims) + (mm(ah, bl, dims) + mm(al, bh, dims))


def d2(a, b, dims):
    ah, al = split(a)
    return mm(ah, b, dims) + mm(al, b, dims)


def d2r(a, b, dims):
    bh, bl = split(b)
    return mm(a, bh, dims) + mm(a, bl, dims)


def row_starts(lens_ref, first_row):
    t = lax.broadcasted_iota(jnp.int32, (ROWS, 1), 0) + first_row
    start = jnp.zeros((ROWS, 1), jnp.int32)
    at = jnp.int32(0)
    for doc in range(NDOCS):
        start = jnp.where(t >= at, at, start)
        at = at + lens_ref[doc]
    return start - first_row


def iotas():
    return (
        lax.broadcasted_iota(jnp.int32, (ROWS, ROWS), 0),
        lax.broadcasted_iota(jnp.int32, (ROWS, ROWS), 1),
    )


def sigmoid(z):
    return 1.0 / (1.0 + jnp.exp(-z))


def unit(z):
    act = z * sigmoid(z)
    scale = lax.rsqrt(jnp.sum(act * act, axis=-1, keepdims=True) + 1e-06)
    return act * scale


def unit_back(z, grad):
    gate = sigmoid(z)
    act = z * gate
    scale = lax.rsqrt(jnp.sum(act * act, axis=-1, keepdims=True) + 1e-06)
    out = act * scale
    act_grad = scale * (grad - out * jnp.sum(out * grad, axis=-1, keepdims=True))
    return act_grad * (gate * (1.0 + z * (1.0 - gate)))


def lower_inverses(lows, ri, ci):
    half = ROWS // 2
    eye = (ri == ci).astype(f32)
    r, c = ri[:half, :half], ci[:half, :half]
    parts = [p for low in lows for p in (low[:half, :half], low[half:, half:])]
    small = eye[:half, :half]
    near = (r >> 1) == (c >> 1)
    invs = [small - jnp.where(near, p, 0.0) for p in parts]
    parts = [p.astype(bf16) for p in parts]
    for k in range(1, 7):
        ring = ((r >> (k + 1)) == (c >> (k + 1))) & ((r >> k) != (c >> k))
        inv16 = [inv.astype(bf16) for inv in invs]
        mids = [
            mm(jnp.where(ring, p, jnp.zeros_like(p)), i, NN).astype(bf16)
            for p, i in zip(parts, inv16)
        ]
        invs = [inv - mm(i, mid, NN) for inv, i, mid in zip(invs, inv16, mids)]
    whole = []
    for n, low in enumerate(lows):
        top, bottom = invs[2 * n], invs[2 * n + 1]
        corner = -d1(d1(bottom, low[half:, :half], NN), top, NN)
        upper = jnp.concatenate([top, jnp.zeros((half, half), f32)], axis=1)
        lower = jnp.concatenate([corner, bottom], axis=1)
        whole.append(jnp.concatenate([upper, lower], axis=0))
    misses = [(eye - inv) - d3(low, inv, NN) for low, inv in zip(lows, whole)]
    return [inv + d1(inv, miss, NN) for inv, miss in zip(whole, misses)]


def kept(lens_ref, i):
    start = jnp.int32(0)
    at = jnp.int32(0)
    for doc in range(NDOCS):
        start = jnp.where((i + 1) * ROWS > at, at, start)
        at = at + lens_ref[doc]
    return jnp.where(start < i * ROWS, 1.0, 0.0).astype(f32)


def signal_all(peers):
    barrier = pltpu.get_barrier_semaphore()
    for axis, index in peers:
        pl.semaphore_signal(barrier, inc=1, device_id={axis: index}, device_id_type=MESH)
    pl.semaphore_wait(barrier, len(peers))


def seq_peers(me):
    return [("seq", lax.rem(me + hop, SEQ)) for hop in range(1, SEQ)]


def remote(source, target, send_sem, recv_sem, peer, axis="seq"):
    return pltpu.make_async_remote_copy(
        src_ref=source,
        dst_ref=target,
        send_sem=send_sem,
        recv_sem=recv_sem,
        device_id={axis: peer},
        device_id_type=MESH,
    )


def spread(me, source, target, sems, peers):
    send, recv = sems
    for peer in peers:

        @pl.when(peer != me)
        def _(peer=peer):
            remote(source.at[peer], target.at[me], send.at[peer], recv.at[me], peer).start()


def team_peers(me, team):
    return [team * 8 + lax.rem(me + n, 8) for n in range(8)]


def settle(me, source, target, sems):
    send, recv = sems
    for hop in range(1, SEQ):
        peer = lax.rem(me + hop, SEQ)
        remote(source.at[peer], target.at[peer], send.at[peer], recv.at[peer], peer).wait()


def share(me, source, target, sems):
    send, recv = sems
    for hop in range(1, SEQ):
        peer = lax.rem(me + hop, SEQ)
        remote(source, target.at[me], send.at[peer], recv.at[me], peer).start()


def settle_share(me, source, target, sems):
    send, recv = sems
    for hop in range(1, SEQ):
        peer = lax.rem(me + hop, SEQ)
        remote(source, target.at[peer], send.at[peer], recv.at[peer], peer).wait()


def lanes(head):
    return pl.ds(pl.multiple_of(head * HEAD, HEAD), HEAD)


def front_kernel(
    lens_ref, bias_ref, q_ref, k_ref, v_ref, qm_ref, km_ref, bw_ref,
    zq_out, zk_out, beta_out, t_out, w_out, sc_out, qe_out, gap_ref, s_ref, hops_ref,
    zq_ref, zk_ref, beta_ref, t_ref, w_ref, sc_ref, qe_ref, fresh_ref, teacher_ref,
    pa_ref, got, outs, s_in, kv, kk, vv,
    out_sem, kv_send, kv_recv, send1, recv1, send2, recv2,
):
    me = lax.axis_index("seq")
    first = me * ROWS
    k = k_ref[...]
    v16 = v_ref[...]
    v = v16.astype(f32)
    kv[me, :, :HEAD] = k
    kv[me, :, HEAD:] = v16
    signal_all(seq_peers(me))

    def kv_copy(owner, peer):
        return remote(kv.at[owner], kv.at[owner], kv_send.at[peer], kv_recv.at[owner], peer)

    lax.fori_loop(me + 1, SEQ, lambda peer, _: (kv_copy(me, peer).start(), _)[1], 0)

    start = row_starts(lens_ref, first)
    lead = (start < 0).astype(f32)
    lead_last = lead[ROWS - 1 :, :]
    tail = (start == start[ROWS - 1 :, :]).astype(f32)
    ri, ci = iotas()
    allowed = (ci <= ri) & (ci >= start)
    strict = (ci < ri) & (ci >= start)
    team = range(TEAM)

    def prepare(turn, _):
        heads = [turn * TEAM + n for n in team]
        qus, kus, betas = [], [], []
        for h in heads:
            q = q_ref[:, lanes(h)]
            qh, ql = split(qm_ref[h])
            kh, kl = split(km_ref[h])
            zq = mm(q, qh, NN) + mm(q, ql, NN)
            zk = mm(k, kh, NN) + mm(k, kl, NN)
            zq_ref[h] = zq
            zk_ref[h] = zk
            logits = jnp.sum(q.astype(f32) * bw_ref[h], axis=-1, keepdims=True)
            beta = sigmoid(logits + bias_ref[h])
            beta_ref[h] = beta
            qus.append(unit(zq))
            kus.append(unit(zk))
            betas.append(beta)
        lows = [jnp.where(strict, betas[n] * d3(kus[n], kus[n], NT), 0.0) for n in team]
        invs = lower_inverses(lows, ri, ci)
        ws = [
            d3(invs[n], jnp.concatenate([betas[n] * kus[n], betas[n] * v], axis=1), NN)
            for n in team
        ]
        scores = [jnp.where(allowed, d3(qus[n], kus[n], NT), 0.0) for n in team]
        for n, h in enumerate(heads):
            t_ref[h] = invs[n]
            w_ref[h] = ws[n]
            sc_ref[h] = scores[n]
            mixed = d3(scores[n], ws[n], NN)
            qe_ref[h] = qus[n] - mixed[:, :HEAD]
            fresh_ref[h] = mixed[:, HEAD:]
            both = jnp.concatenate([ws[n][:, :HEAD], tail * ws[n][:, HEAD:]], axis=1)
            pair = d3(both, kus[n], TN)
            hop = (-lead_last * pair[:HEAD]).astype(bf16)
            add = pair[HEAD:].astype(bf16)
            for side in range(2):
                pa_ref[2 * h + side, :HEAD] = hop
                pa_ref[2 * h + side, HEAD:] = add[side * (HEAD // 2) : (side + 1) * (HEAD // 2)]
        spread(me, pa_ref, got, (send1, recv1), team_peers(me, turn))
        return _

    lax.fori_loop(0, HEADS // TEAM, prepare, 0)
    kept_arrays = [
        pltpu.make_async_copy(a, b, out_sem.at[n])
        for n, (a, b) in enumerate([
            (zq_ref, zq_out), (zk_ref, zk_out), (beta_ref, beta_out), (t_ref, t_out),
            (w_ref, w_out), (sc_ref, sc_out), (qe_ref, qe_out),
        ])
    ]
    for copy in kept_arrays:
        copy.start()

    def arrive(owner, _):
        kv_copy(owner, owner).wait_recv()
        return _

    lax.fori_loop(0, me, arrive, 0)

    def lay(owner, _):
        at = pl.ds(pl.multiple_of(owner * ROWS, ROWS), ROWS)
        block = kv[owner]
        kk[at, :HEAD] = block[:, :HEAD]
        kk[at, HEAD:] = block[:, :HEAD]
        vv[at, :HEAD] = block[:, HEAD:]
        vv[at, HEAD:] = jnp.ones((ROWS, HEAD), bf16)
        return _

    def blank(owner, _):
        at = pl.ds(pl.multiple_of(owner * ROWS, ROWS), ROWS)
        kk[at, :] = jnp.zeros((ROWS, 2 * HEAD), bf16)
        vv[at, :] = jnp.zeros((ROWS, 2 * HEAD), bf16)
        return _

    lax.fori_loop(0, me + 1, lay, 0)
    lax.fori_loop(me + 1, SEQ, blank, 0)
    scale = math.log2(math.e) / math.sqrt(HEAD)
    row = lax.broadcasted_iota(jnp.int32, (ROWS, 1), 0)
    lane = lax.broadcasted_iota(jnp.int32, (1, KEY_BLOCK), 1)

    def attend(turn):
        queries = []
        for n in team:
            hi, lo = split(q_ref[:, lanes(turn * TEAM + n)].astype(f32) * scale)
            queries.append(jnp.concatenate([hi, lo], axis=1))

        def step(block, carry):
            at = pl.ds(pl.multiple_of(block * KEY_BLOCK, KEY_BLOCK), KEY_BLOCK)
            keys = kk[at, :]
            values = vv[at, :]
            u = lane + (block * KEY_BLOCK - first)
            seen = (u >= start) & (u <= row)
            out = []
            for query, (peak, acc) in zip(queries, carry):
                s = jnp.where(seen, mm(query, keys, NT), -1e30)
                new = jnp.maximum(peak, jnp.max(s, axis=-1, keepdims=True))
                weights = jnp.exp2(s - new).astype(bf16)
                out.append((new, acc * jnp.exp2(peak - new) + mm(weights, values, NN)))
            return tuple(out)

        carry = tuple(
            (jnp.full((ROWS, 1), -1e30, f32), jnp.zeros((ROWS, 2 * HEAD), f32)) for _ in team
        )
        carry = lax.fori_loop(0, (first + ROWS - 1) // KEY_BLOCK + 1, step, carry)
        for n in team:
            acc = carry[n][1]
            teacher_ref[turn * TEAM + n] = acc[:, :HEAD] / acc[:, HEAD : HEAD + 1]

    attend(0)
    got[me] = pa_ref[me]
    settle(me, pa_ref, got, (send1, recv1))

    def advance(i, state):
        outs[i] = state.astype(bf16)
        block = got[i]
        hops_ref[i] = block[:HEAD]
        hop = block[:HEAD]
        return kept(lens_ref, i) * state + d2(state, hop, NN) + block[HEAD:].astype(f32)

    lax.fori_loop(0, SEQ, advance, jnp.zeros((HEAD // 2, HEAD), f32))
    for turn in range(2):
        spread(me, outs, s_in, (send2, recv2), team_peers(me, turn))
    s_in[me] = outs[me]
    attend(1)
    settle(me, outs, s_in, (send2, recv2))
    for h in range(HEADS):
        state = jnp.concatenate([s_in[2 * h], s_in[2 * h + 1]], axis=0)
        s_ref[h] = state
        student = lead * d3(qe_ref[h], state, NT) + fresh_ref[h]
        gap_ref[:, h * HEAD : (h + 1) * HEAD] = (student - teacher_ref[h]).astype(bf16)
    lax.fori_loop(me + 1, SEQ, lambda peer, _: (kv_copy(me, peer).wait_send(), _)[1], 0)
    for copy in kept_arrays:
        copy.wait()


def tail_kernel(
    lens_ref, gap_ref, q_ref, k_ref, v_ref, s_ref, hops_ref,
    proj_ref, zq_in, zk_in, beta_in, t_in, w_in, sc_in, qe_in,
    dq_ref, dk_ref, row_ref, loss_out,
    zq_ref, zk_ref, beta_ref, t_ref, w_ref, sc_ref, qe_ref, grad_ref, loss_ref,
    ds_ref, ds_got, outs, lam_ref, pq, pq_got, pq_own, pq_all, pk, pk_got, pk_own, pk_all,
    w, sib_out, sib_in, far, up, down, in_a, in_b, in_up, in_down, r,
    w_sem, sib_send, sib_recv, rs_send, rs_recv, ag_send, ag_recv, in_sem,
    send1, recv1, send2, recv2, send3, recv3, send4, recv4, send5, recv5, send6, recv6,
):
    me = lax.axis_index("seq")
    head = lax.axis_index("head")
    z, core = head // 2, lax.rem(head, 2)
    zp, zm, z2 = lax.rem(z + 1, 4), lax.rem(z + 3, 4), lax.rem(z + 2, 4)
    above, below, sibling = zp * 2 + core, zm * 2 + core, z * 2 + (1 - core)
    order = (z2, zp, zm, z)

    def weight_copy(side, quarter, half):
        at = side * 8 + quarter * 2 + half
        return pltpu.make_async_copy(
            proj_ref.at[:, pl.ds(pl.multiple_of(at * HALF, HALF), HALF)], w.at[at], w_sem.at[at]
        )

    for side in (1 - core, core):
        for quarter in order:
            for half in range(2):
                weight_copy(side, quarter, half).start()

    kept_arrays = [
        pltpu.make_async_copy(a, b, in_sem.at[n])
        for n, (a, b) in enumerate([
            (qe_in, qe_ref), (zq_in, zq_ref), (zk_in, zk_ref), (w_in, w_ref), (sc_in, sc_ref),
            (beta_in, beta_ref), (t_in, t_ref),
        ])
    ]
    for copy in kept_arrays:
        copy.start()
    signal_all([("head", above), ("head", below), ("head", sibling)] + seq_peers(me))

    def send(source, target, peer, send_sem, recv_sem):
        copy = remote(source, target, send_sem, recv_sem, peer, "head")
        copy.start()
        return copy

    gap = gap_ref[...]

    def part(side, quarter, half):
        weight_copy(side, quarter, half).wait()
        return mm(gap, w[side * 8 + quarter * 2 + half], NN)

    sib = []
    for n, quarter in enumerate(order):
        for half in range(2):
            sib_out[n, half] = part(1 - core, quarter, half).astype(bf16)
        sib.append(send(sib_out.at[n], sib_in.at[n], sibling, sib_send.at[n], sib_recv.at[n]))

    def pair(n, half):
        return part(core, order[n], half) + sib_in[n, half].astype(f32)

    sib[0].wait_recv()
    far[0] = pair(0, 0).astype(bf16)
    send_a = send(far.at[0], in_a, above, rs_send.at[0], rs_recv.at[0])
    far[1] = pair(0, 1).astype(bf16)
    send_b = send(far.at[1], in_b, below, rs_send.at[1], rs_recv.at[1])
    sib[1].wait_recv()
    up[1] = pair(1, 1).astype(bf16)
    first_up = pair(1, 0)
    send_a.wait_recv()
    up[0] = (first_up + in_a[...].astype(f32)).astype(bf16)
    send_up = send(up, in_up, above, rs_send.at[2], rs_recv.at[2])
    sib[2].wait_recv()
    down[0] = pair(2, 0).astype(bf16)
    first_down = pair(2, 1)
    send_b.wait_recv()
    down[1] = (first_down + in_b[...].astype(f32)).astype(bf16)
    send_down = send(down, in_down, below, rs_send.at[3], rs_recv.at[3])
    sib[3].wait_recv()
    mine = [pair(3, 0), pair(3, 1)]
    send_up.wait_recv()
    send_down.wait_recv()
    own = core * 4 + z
    for half in range(2):
        total = mine[half] + (in_up[half].astype(f32) + in_down[half].astype(f32))
        r[own, half] = total.astype(bf16)

    def gather(chunk, half, peer, n):
        ref = r.at[chunk] if half is None else r.at[chunk, half]
        return send(ref, ref, peer, ag_send.at[n], ag_recv.at[n])

    loss_ref[...] = jnp.zeros_like(loss_ref)

    def use(chunk, half, first=False):
        block = r[chunk, half]
        term = 2.0 * mm(block, w[chunk * 2 + half], NT)
        grad_ref[...] = term if first else grad_ref[...] + term
        wide = block.astype(f32)
        loss_ref[...] += jnp.sum(wide * wide, axis=0, keepdims=True)

    sides = core * 4
    others = (1 - core) * 4
    own_up = gather(own, None, above, 0)
    own_down = gather(own, None, below, 1)
    own_sib = gather(own, None, sibling, 2)
    use(own, 0, True)
    use(own, 1)
    own_sib.wait_recv()
    use(others + z, 0)
    use(others + z, 1)
    own_up.wait_recv()
    pass_a = gather(sides + zm, 0, above, 3)
    sib_m = gather(sides + zm, None, sibling, 4)
    own_down.wait_recv()
    pass_b = gather(sides + zp, 1, below, 5)
    sib_p = gather(sides + zp, None, sibling, 6)
    use(sides + zm, 0)
    use(sides + zm, 1)
    use(sides + zp, 0)
    use(sides + zp, 1)
    sib_m.wait_recv()
    use(others + zm, 0)
    use(others + zm, 1)
    sib_p.wait_recv()
    use(others + zp, 0)
    use(others + zp, 1)
    pass_a.wait_recv()
    sib_a = gather(sides + z2, 0, sibling, 7)
    pass_b.wait_recv()
    sib_b = gather(sides + z2, 1, sibling, 8)
    use(sides + z2, 0)
    use(sides + z2, 1)
    sib_a.wait_recv()
    use(others + z2, 0)
    sib_b.wait_recv()
    use(others + z2, 1)
    for copy in sib + [
        send_a, send_b, send_up, send_down, own_up, own_down, own_sib,
        pass_a, sib_m, pass_b, sib_p, sib_a, sib_b,
    ]:
        copy.wait_send()
    for copy in kept_arrays:
        copy.wait()

    start = row_starts(lens_ref, me * ROWS)
    lead = (start < 0).astype(f32)
    lead_last = lead[ROWS - 1 :, :]
    tail = (start == start[ROWS - 1 :, :]).astype(f32)
    ri, ci = iotas()
    allowed = (ci <= ri) & (ci >= start)
    strict = (ci < ri) & (ci >= start)
    team = range(TEAM)
    half = HEAD // 2

    def state_grads(turn, _):
        for n in team:
            h = turn * TEAM + n
            ds = d3(lead * grad_ref[:, lanes(h)], qe_ref[h], TN).astype(bf16)
            ds_ref[2 * h] = ds[:half]
            ds_ref[2 * h + 1] = ds[half:]
        spread(me, ds_ref, ds_got, (send1, recv1), team_peers(me, turn))
        return _

    lax.fori_loop(0, HEADS // TEAM, state_grads, 0)

    def query_side(turn, _):
        heads = [turn * TEAM + n for n in team]
        gs = [grad_ref[:, lanes(h)] for h in heads]
        dqes = [d3(lead * g, s_ref[h], NN) for h, g in zip(heads, gs)]
        boths = [jnp.concatenate([-dqe, g], axis=1) for dqe, g in zip(dqes, gs)]
        dscs = [jnp.where(allowed, d3(b, w_ref[h], NT), 0.0) for h, b in zip(heads, boths)]
        for h, both in zip(heads, boths):
            sc_ref[h] = d3(sc_ref[h], both, TN)
        for n, h in enumerate(heads):
            zq = zq_ref[h]
            qe_ref[h] = d3(dscs[n], unit(zq), TN)
            dqu = dqes[n] + d3(dscs[n], unit(zk_ref[h]), NN)
            dqm = d2r(q_ref[:, lanes(h)], unit_back(zq, dqu), TN)
            pq[2 * h] = dqm[:half]
            pq[2 * h + 1] = dqm[half:]
        spread(me, pq, pq_got, (send3, recv3), team_peers(me, turn))
        return _

    lax.fori_loop(0, HEADS // TEAM, query_side, 0)
    ds_got[me] = ds_ref[me]
    settle(me, ds_ref, ds_got, (send1, recv1))

    def retreat(n, state):
        i = SEQ - 1 - n
        outs[i] = state.astype(bf16)
        return kept(lens_ref, i) * state + d2(state, hops_ref[i], NT) + ds_got[i].astype(f32)

    lax.fori_loop(0, SEQ, retreat, jnp.zeros((half, HEAD), f32))
    for turn in range(2):
        spread(me, outs, lam_ref, (send2, recv2), team_peers(me, turn))
    lam_ref[me] = outs[me]

    pq_got[me] = pq[me]
    settle(me, pq, pq_got, (send3, recv3))
    pq_own[...] = lax.fori_loop(
        0, SEQ, lambda i, total: total + pq_got[i], jnp.zeros((half, HEAD), f32)
    ).astype(bf16)
    share(me, pq_own, pq_all, (send4, recv4))
    pq_all[me] = pq_own[...]
    settle(me, outs, lam_ref, (send2, recv2))

    k = k_ref[...]
    v = v_ref[...].astype(f32)
    loss = jnp.broadcast_to(jnp.sum(loss_ref[...], axis=1, keepdims=True), (1, HEAD))

    def key_side(turn, _):
        heads = [turn * TEAM + n for n in team]
        lams = [jnp.concatenate([lam_ref[2 * h], lam_ref[2 * h + 1]], axis=0) for h in heads]
        kus = [unit(zk_ref[h]) for h in heads]
        ws = [w_ref[h] for h in heads]
        dhops = [lead_last * mm(s_ref[h], lams[n], TN) for n, h in enumerate(heads)]
        drs = []
        for n, h in enumerate(heads):
            dwk = sc_ref[h, :, :HEAD] - d3(kus[n], dhops[n], NT)
            dwv = sc_ref[h, :, HEAD:] + tail * d2(kus[n], lams[n], NT)
            drs.append(d3(t_ref[h], jnp.concatenate([dwk, dwv], axis=1), TN))
        dkus = [
            qe_ref[h]
            - d3(ws[n][:, :HEAD], dhops[n], NN)
            + tail * d2(ws[n][:, HEAD:], lams[n], NN)
            for n, h in enumerate(heads)
        ]
        dlows = [jnp.where(strict, -d3(drs[n], ws[n], NT), 0.0) for n in team]
        kterms = [drs[n][:, :HEAD] + d3(dlows[n], kus[n], NN) for n in team]
        for n, h in enumerate(heads):
            beta = beta_ref[h]
            dbeta = jnp.sum(kterms[n] * kus[n] + drs[n][:, HEAD:] * v, axis=-1, keepdims=True)
            dku = dkus[n] + beta * kterms[n] + d3(beta * dlows[n], kus[n], TN)
            dkm = d2r(k, unit_back(zk_ref[h], dku), TN)
            dlogit = dbeta * beta * (1.0 - beta)
            q = q_ref[:, lanes(h)].astype(f32)
            rows = jnp.concatenate(
                [jnp.sum(q * dlogit, axis=0, keepdims=True), loss, jnp.zeros((14, HEAD), f32)],
                axis=0,
            )
            for side in range(2):
                pk[2 * h + side, :half] = dkm[side * half : (side + 1) * half]
                pk[2 * h + side, half:] = rows
        spread(me, pk, pk_got, (send5, recv5), team_peers(me, turn))
        return _

    lax.fori_loop(0, HEADS // TEAM, key_side, 0)
    pk_got[me] = pk[me]
    settle(me, pk, pk_got, (send5, recv5))
    total = lax.fori_loop(
        0, SEQ, lambda i, total: total + pk_got[i], jnp.zeros((half + 16, HEAD), f32)
    )
    pk_own[...] = total.astype(bf16)
    share(me, pk_own, pk_all, (send6, recv6))
    pk_all[me] = pk_own[...]
    loss_out[...] = total[half:]
    settle_share(me, pq_own, pq_all, (send4, recv4))
    dq_ref[...] = pq_all[...]
    settle_share(me, pk_own, pk_all, (send6, recv6))
    dk_ref[...] = pk_all[:, :half]
    row_ref[...] = pk_all[:, half:]


def shape(dims, dtype):
    return jax.ShapeDtypeStruct(dims, dtype)


SMEM = pl.BlockSpec(memory_space=pltpu.SMEM)
VMEM = pl.BlockSpec(memory_space=pltpu.VMEM)
ANY = pl.BlockSpec(memory_space=pl.ANY)


def params(**more):
    return pltpu.CompilerParams(vmem_limit_bytes=VMEM_BYTES, has_side_effects=True, **more)


def shards(q, k, v, lens, proj, query_map, key_map, beta_weight, beta_bias):
    bw = beta_weight.reshape(HEADS, 1, HEAD)
    square = (HEADS, ROWS, ROWS)
    slab = (HEADS, ROWS, HEAD)
    halves = (SEQ, HEAD // 2, HEAD)
    saved = [slab, slab, (HEADS, ROWS, 1), square, square, square, slab]
    sems = pltpu.SemaphoreType.DMA((SEQ,))
    *saved_arrays, gap, state, hops = pl.pallas_call(
        front_kernel,
        in_specs=[SMEM, SMEM] + [VMEM] * 6,
        out_specs=[ANY] * 7 + [VMEM] * 3,
        out_shape=[shape(dims, f32) for dims in saved] + [
            shape((ROWS, HEADS * HEAD), bf16), shape((HEADS, HEAD, HEAD), bf16),
            shape((SEQ, HEAD, HEAD), bf16),
        ],
        scratch_shapes=[pltpu.VMEM(dims, f32) for dims in saved] + [
            pltpu.VMEM(slab, f32),
            pltpu.VMEM(slab, f32),
            pltpu.VMEM((SEQ, 192, HEAD), bf16),
            pltpu.VMEM((SEQ, 192, HEAD), bf16),
            pltpu.VMEM(halves, bf16),
            pltpu.VMEM(halves, bf16),
            pltpu.VMEM((SEQ, ROWS, 2 * HEAD), bf16),
            pltpu.VMEM((SEQ * ROWS, 2 * HEAD), bf16),
            pltpu.VMEM((SEQ * ROWS, 2 * HEAD), bf16),
            pltpu.SemaphoreType.DMA((7,)),
        ] + [sems] * 6,
        compiler_params=params(collective_id=0),
        name="front",
    )(lens, beta_bias, q, k, v, query_map, key_map, bw)

    block = (2, ROWS, HALF)
    extended = (SEQ, HEAD // 2 + 16, HEAD)
    dq, dk, rows, loss = pl.pallas_call(
        tail_kernel,
        in_specs=[SMEM] + [VMEM] * 6 + [ANY] * 8,
        out_specs=[VMEM] * 4,
        out_shape=[
            shape(halves, bf16), shape(halves, bf16), shape((SEQ, 16, HEAD), bf16),
            shape((16, HEAD), f32),
        ],
        scratch_shapes=[pltpu.VMEM(dims, f32) for dims in saved] + [
            pltpu.VMEM((ROWS, HEADS * HEAD), f32),
            pltpu.VMEM((1, HALF), f32),
            pltpu.VMEM(halves, bf16),
            pltpu.VMEM(halves, bf16),
            pltpu.VMEM(halves, bf16),
            pltpu.VMEM(halves, bf16),
            pltpu.VMEM(halves, f32),
            pltpu.VMEM(halves, f32),
            pltpu.VMEM(halves[1:], bf16),
            pltpu.VMEM(halves, bf16),
            pltpu.VMEM(extended, f32),
            pltpu.VMEM(extended, f32),
            pltpu.VMEM(extended[1:], bf16),
            pltpu.VMEM(extended, bf16),
            pltpu.VMEM((16, HEADS * HEAD, HALF), bf16),
            pltpu.VMEM((4,) + block, bf16),
            pltpu.VMEM((4,) + block, bf16),
            pltpu.VMEM(block, bf16),
            pltpu.VMEM(block, bf16),
            pltpu.VMEM(block, bf16),
            pltpu.VMEM(block[1:], bf16),
            pltpu.VMEM(block[1:], bf16),
            pltpu.VMEM(block, bf16),
            pltpu.VMEM(block, bf16),
            pltpu.VMEM((8,) + block, bf16),
            pltpu.SemaphoreType.DMA((16,)),
            pltpu.SemaphoreType.DMA((4,)),
            pltpu.SemaphoreType.DMA((4,)),
            pltpu.SemaphoreType.DMA((4,)),
            pltpu.SemaphoreType.DMA((4,)),
            pltpu.SemaphoreType.DMA((9,)),
            pltpu.SemaphoreType.DMA((9,)),
            pltpu.SemaphoreType.DMA((7,)),
        ] + [sems] * 12,
        compiler_params=params(collective_id=1),
        name="tail",
    )(lens, gap, q, k, v, state, hops, proj, *saved_arrays)
    match_loss = loss[1, 0] / (SEQ * ROWS * WIDTH)
    grad_query = dq.astype(f32).reshape(HEADS, HEAD, HEAD)
    grad_key = dk.astype(f32).reshape(HEADS, HEAD, HEAD)
    grad_beta = rows[::2, 0].astype(f32)
    return match_loss, grad_query, grad_key, grad_beta


def solution(mesh):
    return jax.shard_map(
        shards,
        mesh=mesh,
        in_specs=(
            P("seq", "head"),
            P("seq", "head"),
            P("seq", "head"),
            P(),
            P("head", None),
            P("head", None, None),
            P("head", None, None),
            P("head", None),
            P("head"),
        ),
        out_specs=(P(), P("head", None, None), P("head", None, None), P("head", None)),
        check_vma=False,
    )
```

```python
import functools
import math

import jax
import jax.numpy as jnp
from jax import lax
from jax.experimental import pallas as pl
from jax.experimental.pallas import tpu as pltpu
from jax.sharding import PartitionSpec as P

HEAD = 128
ROWS = 256
HEADS = 8
SEQ = 16
NDOCS = 8
WIDTH = 8192
HALF = 512
KEY_BLOCK = 2048
TEAM = 4

f32 = jnp.float32
bf16 = jnp.bfloat16
NN = ((1,), (0,))
NT = ((1,), (1,))
TN = ((0,), (0,))
VMEM_BYTES = 56 * 1024 * 1024
MESH = pl.DeviceIdType.MESH


def mm(a, b, dims):
    return lax.dot_general(a, b, (dims, ((), ())), preferred_element_type=f32)


def split(x):
    hi = x.astype(bf16)
    return hi, (x - hi.astype(f32)).astype(bf16)


def d1(a, b, dims):
    return mm(a.astype(bf16), b.astype(bf16), dims)


def d3(a, b, dims):
    ah, al = split(a)
    bh, bl = split(b)
    return mm(ah, bh, dims) + (mm(ah, bl, dims) + mm(al, bh, dims))


def d2(a, b, dims):
    ah, al = split(a)
    return mm(ah, b, dims) + mm(al, b, dims)


def d2r(a, b, dims):
    bh, bl = split(b)
    return mm(a, bh, dims) + mm(a, bl, dims)


def row_starts(lens_ref, first_row):
    t = lax.broadcasted_iota(jnp.int32, (ROWS, 1), 0) + first_row
    start = jnp.zeros((ROWS, 1), jnp.int32)
    at = jnp.int32(0)
    for doc in range(NDOCS):
        start = jnp.where(t >= at, at, start)
        at = at + lens_ref[doc]
    return start - first_row


def iotas():
    return (
        lax.broadcasted_iota(jnp.int32, (ROWS, ROWS), 0),
        lax.broadcasted_iota(jnp.int32, (ROWS, ROWS), 1),
    )


def sigmoid(z):
    return 1.0 / (1.0 + jnp.exp(-z))


def unit(z):
    act = z * sigmoid(z)
    scale = lax.rsqrt(jnp.sum(act * act, axis=-1, keepdims=True) + 1e-06)
    return act * scale


def unit_back(z, grad):
    gate = sigmoid(z)
    act = z * gate
    scale = lax.rsqrt(jnp.sum(act * act, axis=-1, keepdims=True) + 1e-06)
    out = act * scale
    act_grad = scale * (grad - out * jnp.sum(out * grad, axis=-1, keepdims=True))
    return act_grad * (gate * (1.0 + z * (1.0 - gate)))


def lower_inverses(lows, ri, ci):
    half = ROWS // 2
    eye = (ri == ci).astype(f32)
    r, c = ri[:half, :half], ci[:half, :half]
    parts = [p for low in lows for p in (low[:half, :half], low[half:, half:])]
    small = eye[:half, :half]
    near = (r >> 1) == (c >> 1)
    invs = [small - jnp.where(near, p, 0.0) for p in parts]
    parts = [p.astype(bf16) for p in parts]
    for k in range(1, 7):
        ring = ((r >> (k + 1)) == (c >> (k + 1))) & ((r >> k) != (c >> k))
        inv16 = [inv.astype(bf16) for inv in invs]
        mids = [
            mm(jnp.where(ring, p, jnp.zeros_like(p)), i, NN).astype(bf16)
            for p, i in zip(parts, inv16)
        ]
        invs = [inv - mm(i, mid, NN) for inv, i, mid in zip(invs, inv16, mids)]
    whole = []
    for n, low in enumerate(lows):
        top, bottom = invs[2 * n], invs[2 * n + 1]
        corner = -d1(d1(bottom, low[half:, :half], NN), top, NN)
        upper = jnp.concatenate([top, jnp.zeros((half, half), f32)], axis=1)
        lower = jnp.concatenate([corner, bottom], axis=1)
        whole.append(jnp.concatenate([upper, lower], axis=0))
    misses = [(eye - inv) - d3(low, inv, NN) for low, inv in zip(lows, whole)]
    return [inv + d1(inv, miss, NN) for inv, miss in zip(whole, misses)]


def kept(lens_ref, i):
    start = jnp.int32(0)
    at = jnp.int32(0)
    for doc in range(NDOCS):
        start = jnp.where((i + 1) * ROWS > at, at, start)
        at = at + lens_ref[doc]
    return jnp.where(start < i * ROWS, 1.0, 0.0).astype(f32)


def signal_all(peers):
    barrier = pltpu.get_barrier_semaphore()
    for axis, index in peers:
        pl.semaphore_signal(barrier, inc=1, device_id={axis: index}, device_id_type=MESH)
    pl.semaphore_wait(barrier, len(peers))


def seq_peers(me):
    return [("seq", lax.rem(me + hop, SEQ)) for hop in range(1, SEQ)]


def remote(source, target, send_sem, recv_sem, peer, axis="seq"):
    return pltpu.make_async_remote_copy(
        src_ref=source,
        dst_ref=target,
        send_sem=send_sem,
        recv_sem=recv_sem,
        device_id={axis: peer},
        device_id_type=MESH,
    )


def spread(me, source, target, sems, peers):
    send, recv = sems
    for peer in peers:

        @pl.when(peer != me)
        def _(peer=peer):
            remote(source.at[peer], target.at[me], send.at[peer], recv.at[me], peer).start()


def team_peers(me, team):
    return [team * 8 + lax.rem(me + n, 8) for n in range(8)]


def settle(me, source, target, sems):
    send, recv = sems
    for hop in range(1, SEQ):
        peer = lax.rem(me + hop, SEQ)
        remote(source.at[peer], target.at[peer], send.at[peer], recv.at[peer], peer).wait()


def share(me, source, target, sems):
    send, recv = sems
    for hop in range(1, SEQ):
        peer = lax.rem(me + hop, SEQ)
        remote(source, target.at[me], send.at[peer], recv.at[me], peer).start()


def settle_share(me, source, target, sems):
    send, recv = sems
    for hop in range(1, SEQ):
        peer = lax.rem(me + hop, SEQ)
        remote(source, target.at[peer], send.at[peer], recv.at[peer], peer).wait()


def lanes(head):
    return pl.ds(pl.multiple_of(head * HEAD, HEAD), HEAD)


def front_kernel(
    lens_ref, bias_ref, q_ref, k_ref, v_ref, qm_ref, km_ref, bw_ref,
    zq_out, zk_out, beta_out, t_out, w_out, sc_out, qe_out, gap_ref, s_ref, hops_ref,
    zq_ref, zk_ref, beta_ref, t_ref, w_ref, sc_ref, qe_ref, fresh_ref, teacher_ref,
    pa_ref, got, outs, s_in, keys_at, values_at, kk, vv,
    out_sem, kv_send, kv_recv, send1, recv1, send2, recv2,
):
    me = lax.axis_index("seq")
    first = me * ROWS
    k = k_ref[...]
    v16 = v_ref[...]
    v = v16.astype(f32)
    x, y = me // 4, lax.rem(me, 4)
    xp, xm, yp, ym = lax.rem(x + 1, 4), lax.rem(x + 3, 4), lax.rem(y + 1, 4), lax.rem(y + 3, 4)
    keys_at[x, y] = k
    values_at[y, x] = v16
    signal_all(seq_peers(me))

    def relay(n, source, peer):
        return remote(source, source, kv_send.at[n], kv_recv.at[n], peer)

    across = []
    for d in range(1, 4):
        across.append(relay(d - 1, keys_at.at[x, y], x * 4 + lax.rem(y + d, 4)))
        across.append(relay(d + 2, values_at.at[y, x], lax.rem(x + d, 4) * 4 + y))
    whole_rows = [
        relay(6, keys_at.at[x], xp * 4 + y),
        relay(7, keys_at.at[x], xm * 4 + y),
        relay(8, values_at.at[y], x * 4 + yp),
        relay(9, values_at.at[y], x * 4 + ym),
    ]
    far_rows = [
        relay(10, keys_at.at[xm, pl.ds(0, 2)], xp * 4 + y),
        relay(11, keys_at.at[xp, pl.ds(2, 2)], xm * 4 + y),
        relay(12, values_at.at[ym, pl.ds(0, 2)], x * 4 + yp),
        relay(13, values_at.at[yp, pl.ds(2, 2)], x * 4 + ym),
    ]
    for copy in across:
        copy.start()

    def pass_on(turn):
        @pl.when(turn == 0)
        def _():
            for copy in across:
                copy.wait_recv()
            for copy in whole_rows:
                copy.start()

        @pl.when(turn == 1)
        def _():
            for copy in whole_rows:
                copy.wait_recv()
            for copy in far_rows:
                copy.start()

    start = row_starts(lens_ref, first)
    lead = (start < 0).astype(f32)
    lead_last = lead[ROWS - 1 :, :]
    tail = (start == start[ROWS - 1 :, :]).astype(f32)
    ri, ci = iotas()
    allowed = (ci <= ri) & (ci >= start)
    strict = (ci < ri) & (ci >= start)
    team = range(TEAM)

    def prepare(turn, _):
        heads = [turn * TEAM + n for n in team]
        qus, kus, betas = [], [], []
        for h in heads:
            q = q_ref[:, lanes(h)]
            qh, ql = split(qm_ref[h])
            kh, kl = split(km_ref[h])
            zq = mm(q, qh, NN) + mm(q, ql, NN)
            zk = mm(k, kh, NN) + mm(k, kl, NN)
            zq_ref[h] = zq
            zk_ref[h] = zk
            logits = jnp.sum(q.astype(f32) * bw_ref[h], axis=-1, keepdims=True)
            beta = sigmoid(logits + bias_ref[h])
            beta_ref[h] = beta
            qus.append(unit(zq))
            kus.append(unit(zk))
            betas.append(beta)
        lows = [jnp.where(strict, betas[n] * d3(kus[n], kus[n], NT), 0.0) for n in team]
        invs = lower_inverses(lows, ri, ci)
        pass_on(turn)
        ws = [
            d3(invs[n], jnp.concatenate([betas[n] * kus[n], betas[n] * v], axis=1), NN)
            for n in team
        ]
        scores = [jnp.where(allowed, d3(qus[n], kus[n], NT), 0.0) for n in team]
        for n, h in enumerate(heads):
            t_ref[h] = invs[n]
            w_ref[h] = ws[n]
            sc_ref[h] = scores[n]
            mixed = d3(scores[n], ws[n], NN)
            qe_ref[h] = qus[n] - mixed[:, :HEAD]
            fresh_ref[h] = mixed[:, HEAD:]
            both = jnp.concatenate([ws[n][:, :HEAD], tail * ws[n][:, HEAD:]], axis=1)
            pair = d3(both, kus[n], TN)
            hop = (-lead_last * pair[:HEAD]).astype(bf16)
            add = pair[HEAD:].astype(bf16)
            for side in range(2):
                pa_ref[2 * h + side, :HEAD] = hop
                pa_ref[2 * h + side, HEAD:] = add[side * (HEAD // 2) : (side + 1) * (HEAD // 2)]
        spread(me, pa_ref, got, (send1, recv1), team_peers(me, turn))
        return _

    lax.fori_loop(0, HEADS // TEAM, prepare, 0)
    kept_arrays = [
        pltpu.make_async_copy(a, b, out_sem.at[n])
        for n, (a, b) in enumerate([
            (zq_ref, zq_out), (zk_ref, zk_out), (beta_ref, beta_out), (t_ref, t_out),
            (w_ref, w_out), (sc_ref, sc_out), (qe_ref, qe_out),
        ])
    ]
    for copy in kept_arrays:
        copy.start()

    for copy in far_rows:
        copy.wait_recv()
    for at in range(4):
        for n in range(4):
            rows = slice((at * 4 + n) * ROWS, (at * 4 + n + 1) * ROWS)
            block = keys_at[at, n]
            kk[rows, :HEAD] = block
            kk[rows, HEAD:] = block
            vv[rows, :HEAD] = values_at[n, at]
            vv[rows, HEAD:] = jnp.ones((ROWS, HEAD), bf16)
    scale = math.log2(math.e) / math.sqrt(HEAD)
    row = lax.broadcasted_iota(jnp.int32, (ROWS, 1), 0)
    lane = lax.broadcasted_iota(jnp.int32, (1, KEY_BLOCK), 1)

    def attend(turn):
        queries = []
        for n in team:
            hi, lo = split(q_ref[:, lanes(turn * TEAM + n)].astype(f32) * scale)
            queries.append(jnp.concatenate([hi, lo], axis=1))

        def step(block, carry):
            at = pl.ds(pl.multiple_of(block * KEY_BLOCK, KEY_BLOCK), KEY_BLOCK)
            keys = kk[at, :]
            values = vv[at, :]
            u = lane + (block * KEY_BLOCK - first)
            seen = (u >= start) & (u <= row)
            out = []
            for query, (peak, acc) in zip(queries, carry):
                s = jnp.where(seen, mm(query, keys, NT), -1e30)
                new = jnp.maximum(peak, jnp.max(s, axis=-1, keepdims=True))
                weights = jnp.exp2(s - new).astype(bf16)
                out.append((new, acc * jnp.exp2(peak - new) + mm(weights, values, NN)))
            return tuple(out)

        carry = tuple(
            (jnp.full((ROWS, 1), -1e30, f32), jnp.zeros((ROWS, 2 * HEAD), f32)) for _ in team
        )
        carry = lax.fori_loop(0, (first + ROWS - 1) // KEY_BLOCK + 1, step, carry)
        for n in team:
            acc = carry[n][1]
            teacher_ref[turn * TEAM + n] = acc[:, :HEAD] / acc[:, HEAD : HEAD + 1]

    attend(0)
    got[me] = pa_ref[me]
    settle(me, pa_ref, got, (send1, recv1))

    keeps = [kept(lens_ref, i) for i in range(SEQ)]
    state = jnp.zeros((HEAD // 2, HEAD), f32)
    for i in range(SEQ):
        outs[i] = state.astype(bf16)
        block = got[i]
        hops_ref[i] = block[:HEAD]
        hop = block[:HEAD]
        state = keeps[i] * state + d2(state, hop, NN) + block[HEAD:].astype(f32)
    for turn in range(2):
        spread(me, outs, s_in, (send2, recv2), team_peers(me, turn))
    s_in[me] = outs[me]
    attend(1)
    settle(me, outs, s_in, (send2, recv2))
    for h in range(HEADS):
        state = jnp.concatenate([s_in[2 * h], s_in[2 * h + 1]], axis=0)
        s_ref[h] = state
        student = lead * d3(qe_ref[h], state, NT) + fresh_ref[h]
        gap_ref[:, h * HEAD : (h + 1) * HEAD] = (student - teacher_ref[h]).astype(bf16)
    for copy in across + whole_rows + far_rows:
        copy.wait_send()
    for copy in kept_arrays:
        copy.wait()


def tail_kernel(
    lens_ref, gap_ref, q_ref, k_ref, v_ref, s_ref, hops_ref,
    proj_ref, zq_in, zk_in, beta_in, t_in, w_in, sc_in, qe_in,
    dq_ref, dk_ref, row_ref, loss_out,
    zq_ref, zk_ref, beta_ref, t_ref, w_ref, sc_ref, qe_ref, grad_ref, loss_ref,
    ds_ref, ds_got, outs, lam_ref, pq, pq_got, pq_own, pq_all, pk, pk_got, pk_own, pk_all,
    w, sib_out, sib_in, far, up, down, in_a, in_b, in_up, in_down, r,
    w_sem, sib_send, sib_recv, rs_send, rs_recv, ag_send, ag_recv, in_sem,
    send1, recv1, send2, recv2, send3, recv3, send4, recv4, send5, recv5, send6, recv6,
    send7, recv7, send8, recv8,
):
    me = lax.axis_index("seq")
    head = lax.axis_index("head")
    z, core = head // 2, lax.rem(head, 2)
    zp, zm, z2 = lax.rem(z + 1, 4), lax.rem(z + 3, 4), lax.rem(z + 2, 4)
    above, below, sibling = zp * 2 + core, zm * 2 + core, z * 2 + (1 - core)
    order = (z2, zp, zm, z)

    def weight_copy(side, quarter, half):
        at = side * 8 + quarter * 2 + half
        return pltpu.make_async_copy(
            proj_ref.at[:, pl.ds(pl.multiple_of(at * HALF, HALF), HALF)], w.at[at], w_sem.at[at]
        )

    for side in (1 - core, core):
        for quarter in order:
            for half in range(2):
                weight_copy(side, quarter, half).start()

    kept_arrays = [
        pltpu.make_async_copy(a, b, in_sem.at[n])
        for n, (a, b) in enumerate([
            (qe_in, qe_ref), (zq_in, zq_ref), (zk_in, zk_ref), (w_in, w_ref), (sc_in, sc_ref),
            (beta_in, beta_ref), (t_in, t_ref),
        ])
    ]
    for copy in kept_arrays:
        copy.start()
    signal_all([("head", above), ("head", below), ("head", sibling)] + seq_peers(me))

    def send(source, target, peer, send_sem, recv_sem):
        copy = remote(source, target, send_sem, recv_sem, peer, "head")
        copy.start()
        return copy

    gap = gap_ref[...]

    def part(side, quarter, half):
        weight_copy(side, quarter, half).wait()
        return mm(gap, w[side * 8 + quarter * 2 + half], NN)

    sib = []
    for n, quarter in enumerate(order):
        for half in range(2):
            sib_out[n, half] = part(1 - core, quarter, half).astype(bf16)
        sib.append(send(sib_out.at[n], sib_in.at[n], sibling, sib_send.at[n], sib_recv.at[n]))

    def pair(n, half):
        return part(core, order[n], half) + sib_in[n, half].astype(f32)

    sib[0].wait_recv()
    far[0] = pair(0, 0).astype(bf16)
    send_a = send(far.at[0], in_a, above, rs_send.at[0], rs_recv.at[0])
    far[1] = pair(0, 1).astype(bf16)
    send_b = send(far.at[1], in_b, below, rs_send.at[1], rs_recv.at[1])
    sib[1].wait_recv()
    up[1] = pair(1, 1).astype(bf16)
    first_up = pair(1, 0)
    send_a.wait_recv()
    up[0] = (first_up + in_a[...].astype(f32)).astype(bf16)
    send_up = send(up, in_up, above, rs_send.at[2], rs_recv.at[2])
    sib[2].wait_recv()
    down[0] = pair(2, 0).astype(bf16)
    first_down = pair(2, 1)
    send_b.wait_recv()
    down[1] = (first_down + in_b[...].astype(f32)).astype(bf16)
    send_down = send(down, in_down, below, rs_send.at[3], rs_recv.at[3])
    sib[3].wait_recv()
    mine = [pair(3, 0), pair(3, 1)]
    send_up.wait_recv()
    send_down.wait_recv()
    own = core * 4 + z
    for half in range(2):
        total = mine[half] + (in_up[half].astype(f32) + in_down[half].astype(f32))
        r[own, half] = total.astype(bf16)

    def gather(chunk, half, peer, n):
        ref = r.at[chunk] if half is None else r.at[chunk, half]
        return send(ref, ref, peer, ag_send.at[n], ag_recv.at[n])

    loss_ref[...] = jnp.zeros_like(loss_ref)

    def use(chunk, half, first=False):
        block = r[chunk, half]
        term = 2.0 * mm(block, w[chunk * 2 + half], NT)
        grad_ref[...] = term if first else grad_ref[...] + term
        wide = block.astype(f32)
        loss_ref[...] += jnp.sum(wide * wide, axis=0, keepdims=True)

    sides = core * 4
    others = (1 - core) * 4
    own_up = gather(own, None, above, 0)
    own_down = gather(own, None, below, 1)
    own_sib = gather(own, None, sibling, 2)
    use(own, 0, True)
    use(own, 1)
    own_sib.wait_recv()
    use(others + z, 0)
    use(others + z, 1)
    own_up.wait_recv()
    pass_a = gather(sides + zm, 0, above, 3)
    sib_m = gather(sides + zm, None, sibling, 4)
    own_down.wait_recv()
    pass_b = gather(sides + zp, 1, below, 5)
    sib_p = gather(sides + zp, None, sibling, 6)
    use(sides + zm, 0)
    use(sides + zm, 1)
    use(sides + zp, 0)
    use(sides + zp, 1)
    sib_m.wait_recv()
    use(others + zm, 0)
    use(others + zm, 1)
    sib_p.wait_recv()
    use(others + zp, 0)
    use(others + zp, 1)
    pass_a.wait_recv()
    sib_a = gather(sides + z2, 0, sibling, 7)
    pass_b.wait_recv()
    sib_b = gather(sides + z2, 1, sibling, 8)
    use(sides + z2, 0)
    use(sides + z2, 1)
    sib_a.wait_recv()
    use(others + z2, 0)
    sib_b.wait_recv()
    use(others + z2, 1)
    for copy in sib + [
        send_a, send_b, send_up, send_down, own_up, own_down, own_sib,
        pass_a, sib_m, pass_b, sib_p, sib_a, sib_b,
    ]:
        copy.wait_send()
    for copy in kept_arrays:
        copy.wait()

    start = row_starts(lens_ref, me * ROWS)
    lead = (start < 0).astype(f32)
    lead_last = lead[ROWS - 1 :, :]
    tail = (start == start[ROWS - 1 :, :]).astype(f32)
    ri, ci = iotas()
    allowed = (ci <= ri) & (ci >= start)
    strict = (ci < ri) & (ci >= start)
    team = range(TEAM)
    half = HEAD // 2

    def state_grads(turn, _):
        for n in team:
            h = turn * TEAM + n
            ds = d3(lead * grad_ref[:, lanes(h)], qe_ref[h], TN).astype(bf16)
            ds_ref[2 * h] = ds[:half]
            ds_ref[2 * h + 1] = ds[half:]
        spread(me, ds_ref, ds_got, (send1, recv1), team_peers(me, turn))
        return _

    lax.fori_loop(0, HEADS // TEAM, state_grads, 0)

    def query_side(turn, _):
        heads = [turn * TEAM + n for n in team]
        gs = [grad_ref[:, lanes(h)] for h in heads]
        dqes = [d3(lead * g, s_ref[h], NN) for h, g in zip(heads, gs)]
        boths = [jnp.concatenate([-dqe, g], axis=1) for dqe, g in zip(dqes, gs)]
        dscs = [jnp.where(allowed, d3(b, w_ref[h], NT), 0.0) for h, b in zip(heads, boths)]
        for h, both in zip(heads, boths):
            sc_ref[h] = d3(sc_ref[h], both, TN)
        for n, h in enumerate(heads):
            zq = zq_ref[h]
            qe_ref[h] = d3(dscs[n], unit(zq), TN)
            dqu = dqes[n] + d3(dscs[n], unit(zk_ref[h]), NN)
            dqm = d2r(q_ref[:, lanes(h)], unit_back(zq, dqu), TN)
            pq[2 * h] = dqm[:half]
            pq[2 * h + 1] = dqm[half:]
        return _

    query_side(0, 0)
    ds_got[me] = ds_ref[me]
    settle(me, ds_ref, ds_got, (send1, recv1))

    keeps = [kept(lens_ref, i) for i in range(SEQ)]
    state = jnp.zeros((half, HEAD), f32)
    for i in reversed(range(SEQ)):
        outs[i] = state.astype(bf16)
        state = keeps[i] * state + d2(state, hops_ref[i], NT) + ds_got[i].astype(f32)
    for turn in range(2):
        spread(me, outs, lam_ref, (send2, recv2), team_peers(me, turn))
    lam_ref[me] = outs[me]
    query_side(1, 0)
    spread(me, pq, pq_got, (send3, recv3), [p for _, p in seq_peers(me)])

    settle(me, outs, lam_ref, (send2, recv2))

    k = k_ref[...]
    v = v_ref[...].astype(f32)
    loss = jnp.broadcast_to(jnp.sum(loss_ref[...], axis=1, keepdims=True), (1, HEAD))

    key_sems = [(send5, recv5), (send7, recv7)]
    share_sems = [(send6, recv6), (send8, recv8)]

    def key_total(turn):
        pk_got[turn, me] = pk[turn, me]
        settle(me, pk.at[turn], pk_got.at[turn], key_sems[turn])
        total = pk_got[turn, 0]
        for i in range(1, SEQ):
            total = total + pk_got[turn, i]
        pk_own[turn] = total[:32].astype(bf16)
        row_ref[turn * TEAM : (turn + 1) * TEAM] = total[32:36]
        share(me, pk_own.at[turn], pk_all.at[turn], share_sems[turn])
        pk_all[turn, me] = pk_own[turn]
        return total

    def key_side(turn):
        heads = [turn * TEAM + n for n in team]
        lams = [jnp.concatenate([lam_ref[2 * h], lam_ref[2 * h + 1]], axis=0) for h in heads]
        kus = [unit(zk_ref[h]) for h in heads]
        ws = [w_ref[h] for h in heads]
        dhops = [lead_last * mm(s_ref[h], lams[n], TN) for n, h in enumerate(heads)]
        drs = []
        for n, h in enumerate(heads):
            dwk = sc_ref[h, :, :HEAD] - d3(kus[n], dhops[n], NT)
            dwv = sc_ref[h, :, HEAD:] + tail * d2(kus[n], lams[n], NT)
            drs.append(d3(t_ref[h], jnp.concatenate([dwk, dwv], axis=1), TN))
        dkus = [
            qe_ref[h]
            - d3(ws[n][:, :HEAD], dhops[n], NN)
            + tail * d2(ws[n][:, HEAD:], lams[n], NN)
            for n, h in enumerate(heads)
        ]
        dlows = [jnp.where(strict, -d3(drs[n], ws[n], NT), 0.0) for n in team]
        kterms = [drs[n][:, :HEAD] + d3(dlows[n], kus[n], NN) for n in team]
        dkm_rows, extra = [], []
        for n, h in enumerate(heads):
            beta = beta_ref[h]
            dbeta = jnp.sum(kterms[n] * kus[n] + drs[n][:, HEAD:] * v, axis=-1, keepdims=True)
            dku = dkus[n] + beta * kterms[n] + d3(beta * dlows[n], kus[n], TN)
            dkm = d2r(k, unit_back(zk_ref[h], dku), TN)
            dlogit = dbeta * beta * (1.0 - beta)
            q = q_ref[:, lanes(h)].astype(f32)
            dkm_rows.append(dkm.reshape(SEQ, 8, HEAD))
            extra.append(jnp.sum(q * dlogit, axis=0, keepdims=True))
        extra = jnp.concatenate(extra + [loss, jnp.zeros((3, HEAD), f32)], axis=0)
        pk[turn, :, :32] = jnp.concatenate(dkm_rows, axis=1)
        pk[turn, :, 32:] = jnp.broadcast_to(extra[None], (SEQ, 8, HEAD))
        spread(me, pk.at[turn], pk_got.at[turn], key_sems[turn], [p for _, p in seq_peers(me)])

    key_side(0)
    pq_got[me] = pq[me]
    settle(me, pq, pq_got, (send3, recv3))
    pq_own[...] = lax.fori_loop(
        0, SEQ, lambda i, total: total + pq_got[i], jnp.zeros((half, HEAD), f32)
    ).astype(bf16)
    share(me, pq_own, pq_all, (send4, recv4))
    pq_all[me] = pq_own[...]
    key_side(1)
    key_total(0)
    total = key_total(1)
    loss_out[...] = total[36:37]
    settle_share(me, pq_own, pq_all, (send4, recv4))
    dq_ref[...] = pq_all[...].astype(f32)
    for turn in range(2):
        settle_share(me, pk_own.at[turn], pk_all.at[turn], share_sems[turn])
        for n in range(TEAM):
            h = turn * TEAM + n
            wide = pk_all[turn].astype(f32)
            dk_ref[h] = wide[:, n * 8 : (n + 1) * 8].reshape(HEAD, HEAD)


def shape(dims, dtype):
    return jax.ShapeDtypeStruct(dims, dtype)


SMEM = pl.BlockSpec(memory_space=pltpu.SMEM)
VMEM = pl.BlockSpec(memory_space=pltpu.VMEM)
ANY = pl.BlockSpec(memory_space=pl.ANY)


def params(**more):
    return pltpu.CompilerParams(vmem_limit_bytes=VMEM_BYTES, has_side_effects=True, **more)


def shards(q, k, v, lens, proj, query_map, key_map, beta_weight, beta_bias):
    bw = beta_weight.reshape(HEADS, 1, HEAD)
    square = (HEADS, ROWS, ROWS)
    slab = (HEADS, ROWS, HEAD)
    halves = (SEQ, HEAD // 2, HEAD)
    saved = [slab, slab, (HEADS, ROWS, 1), square, square, square, slab]
    sems = pltpu.SemaphoreType.DMA((SEQ,))
    *saved_arrays, gap, state, hops = pl.pallas_call(
        front_kernel,
        in_specs=[SMEM, SMEM] + [VMEM] * 6,
        out_specs=[ANY] * 7 + [VMEM] * 3,
        out_shape=[shape(dims, f32) for dims in saved] + [
            shape((ROWS, HEADS * HEAD), bf16), shape((HEADS, HEAD, HEAD), bf16),
            shape((SEQ, HEAD, HEAD), bf16),
        ],
        scratch_shapes=[pltpu.VMEM(dims, f32) for dims in saved] + [
            pltpu.VMEM(slab, f32),
            pltpu.VMEM(slab, f32),
            pltpu.VMEM((SEQ, 192, HEAD), bf16),
            pltpu.VMEM((SEQ, 192, HEAD), bf16),
            pltpu.VMEM(halves, bf16),
            pltpu.VMEM(halves, bf16),
            pltpu.VMEM((4, 4, ROWS, HEAD), bf16),
            pltpu.VMEM((4, 4, ROWS, HEAD), bf16),
            pltpu.VMEM((SEQ * ROWS, 2 * HEAD), bf16),
            pltpu.VMEM((SEQ * ROWS, 2 * HEAD), bf16),
            pltpu.SemaphoreType.DMA((7,)),
        ] + [sems] * 6,
        compiler_params=params(collective_id=0),
        name="front",
    )(lens, beta_bias, q, k, v, query_map, key_map, bw)

    block = (2, ROWS, HALF)
    extended = (2, SEQ, 40, HEAD)
    dq, dk, grad_beta, loss = pl.pallas_call(
        tail_kernel,
        in_specs=[SMEM] + [VMEM] * 6 + [ANY] * 8,
        out_specs=[VMEM] * 4,
        out_shape=[
            shape(halves, f32), shape((HEADS, HEAD, HEAD), f32), shape((HEADS, HEAD), f32),
            shape((1, HEAD), f32),
        ],
        scratch_shapes=[pltpu.VMEM(dims, f32) for dims in saved] + [
            pltpu.VMEM((ROWS, HEADS * HEAD), f32),
            pltpu.VMEM((1, HALF), f32),
            pltpu.VMEM(halves, bf16),
            pltpu.VMEM(halves, bf16),
            pltpu.VMEM(halves, bf16),
            pltpu.VMEM(halves, bf16),
            pltpu.VMEM(halves, f32),
            pltpu.VMEM(halves, f32),
            pltpu.VMEM(halves[1:], bf16),
            pltpu.VMEM(halves, bf16),
            pltpu.VMEM(extended, f32),
            pltpu.VMEM(extended, f32),
            pltpu.VMEM((2, 32, HEAD), bf16),
            pltpu.VMEM((2, SEQ, 32, HEAD), bf16),
            pltpu.VMEM((16, HEADS * HEAD, HALF), bf16),
            pltpu.VMEM((4,) + block, bf16),
            pltpu.VMEM((4,) + block, bf16),
            pltpu.VMEM(block, bf16),
            pltpu.VMEM(block, bf16),
            pltpu.VMEM(block, bf16),
            pltpu.VMEM(block[1:], bf16),
            pltpu.VMEM(block[1:], bf16),
            pltpu.VMEM(block, bf16),
            pltpu.VMEM(block, bf16),
            pltpu.VMEM((8,) + block, bf16),
            pltpu.SemaphoreType.DMA((16,)),
            pltpu.SemaphoreType.DMA((4,)),
            pltpu.SemaphoreType.DMA((4,)),
            pltpu.SemaphoreType.DMA((4,)),
            pltpu.SemaphoreType.DMA((4,)),
            pltpu.SemaphoreType.DMA((9,)),
            pltpu.SemaphoreType.DMA((9,)),
            pltpu.SemaphoreType.DMA((7,)),
        ] + [sems] * 16,
        compiler_params=params(collective_id=1),
        name="tail",
    )(lens, gap, q, k, v, state, hops, proj, *saved_arrays)
    match_loss = loss[0, 0] / (SEQ * ROWS * WIDTH)
    grad_query = dq.reshape(HEADS, HEAD, HEAD)
    return match_loss, grad_query, dk, grad_beta


def solution(mesh):
    return jax.shard_map(
        shards,
        mesh=mesh,
        in_specs=(
            P("seq", "head"),
            P("seq", "head"),
            P("seq", "head"),
            P(),
            P("head", None),
            P("head", None, None),
            P("head", None, None),
            P("head", None),
            P("head"),
        ),
        out_specs=(P(), P("head", None, None), P("head", None, None), P("head", None)),
        check_vma=False,
    )
```

```python
import functools
import math

import jax
import jax.numpy as jnp
from jax import lax
from jax.experimental import pallas as pl
from jax.experimental.pallas import tpu as pltpu
from jax.sharding import PartitionSpec as P

HEAD = 128
ROWS = 256
HEADS = 8
SEQ = 16
NDOCS = 8
WIDTH = 8192
HALF = 512
KEY_BLOCK = 2048
TEAM = 4

f32 = jnp.float32
bf16 = jnp.bfloat16
NN = ((1,), (0,))
NT = ((1,), (1,))
TN = ((0,), (0,))
VMEM_BYTES = 62 * 1024 * 1024
MESH = pl.DeviceIdType.MESH


def mm(a, b, dims):
    return lax.dot_general(a, b, (dims, ((), ())), preferred_element_type=f32)


def split(x):
    hi = x.astype(bf16)
    return hi, (x - hi.astype(f32)).astype(bf16)


def d1(a, b, dims):
    return mm(a.astype(bf16), b.astype(bf16), dims)


def d3(a, b, dims):
    ah, al = split(a)
    bh, bl = split(b)
    return mm(ah, bh, dims) + (mm(ah, bl, dims) + mm(al, bh, dims))


def d2(a, b, dims):
    ah, al = split(a)
    return mm(ah, b, dims) + mm(al, b, dims)


def d2r(a, b, dims):
    bh, bl = split(b)
    return mm(a, bh, dims) + mm(a, bl, dims)


def row_starts(lens_ref, first_row):
    t = lax.broadcasted_iota(jnp.int32, (ROWS, 1), 0) + first_row
    start = jnp.zeros((ROWS, 1), jnp.int32)
    at = jnp.int32(0)
    for doc in range(NDOCS):
        start = jnp.where(t >= at, at, start)
        at = at + lens_ref[doc]
    return start - first_row


def iotas():
    return (
        lax.broadcasted_iota(jnp.int32, (ROWS, ROWS), 0),
        lax.broadcasted_iota(jnp.int32, (ROWS, ROWS), 1),
    )


def sigmoid(z):
    return 1.0 / (1.0 + jnp.exp(-z))


def unit(z):
    act = z * sigmoid(z)
    scale = lax.rsqrt(jnp.sum(act * act, axis=-1, keepdims=True) + 1e-06)
    return act * scale


def unit_back(z, grad):
    gate = sigmoid(z)
    act = z * gate
    scale = lax.rsqrt(jnp.sum(act * act, axis=-1, keepdims=True) + 1e-06)
    out = act * scale
    act_grad = scale * (grad - out * jnp.sum(out * grad, axis=-1, keepdims=True))
    return act_grad * (gate * (1.0 + z * (1.0 - gate)))


def lower_inverses(lows, ri, ci):
    half = ROWS // 2
    eye = (ri == ci).astype(f32)
    r, c = ri[:half, :half], ci[:half, :half]
    parts = [p for low in lows for p in (low[:half, :half], low[half:, half:])]
    small = eye[:half, :half]
    near = (r >> 1) == (c >> 1)
    invs = [small - jnp.where(near, p, 0.0) for p in parts]
    parts = [p.astype(bf16) for p in parts]
    for k in range(1, 7):
        ring = ((r >> (k + 1)) == (c >> (k + 1))) & ((r >> k) != (c >> k))
        inv16 = [inv.astype(bf16) for inv in invs]
        mids = [
            mm(jnp.where(ring, p, jnp.zeros_like(p)), i, NN).astype(bf16)
            for p, i in zip(parts, inv16)
        ]
        invs = [inv - mm(i, mid, NN) for inv, i, mid in zip(invs, inv16, mids)]
    whole = []
    for n, low in enumerate(lows):
        top, bottom = invs[2 * n], invs[2 * n + 1]
        corner = -d1(d1(bottom, low[half:, :half], NN), top, NN)
        upper = jnp.concatenate([top, jnp.zeros((half, half), f32)], axis=1)
        lower = jnp.concatenate([corner, bottom], axis=1)
        whole.append(jnp.concatenate([upper, lower], axis=0))
    misses = [(eye - inv) - d3(low, inv, NN) for low, inv in zip(lows, whole)]
    return [inv + d1(inv, miss, NN) for inv, miss in zip(whole, misses)]


def kept(lens_ref, i):
    start = jnp.int32(0)
    at = jnp.int32(0)
    for doc in range(NDOCS):
        start = jnp.where((i + 1) * ROWS > at, at, start)
        at = at + lens_ref[doc]
    return jnp.where(start < i * ROWS, 1.0, 0.0).astype(f32)


def signal_all(peers):
    barrier = pltpu.get_barrier_semaphore()
    for axis, index in peers:
        pl.semaphore_signal(barrier, inc=1, device_id={axis: index}, device_id_type=MESH)
    pl.semaphore_wait(barrier, len(peers))


def seq_peers(me):
    return [("seq", lax.rem(me + hop, SEQ)) for hop in range(1, SEQ)]


def remote(source, target, send_sem, recv_sem, peer, axis="seq"):
    return pltpu.make_async_remote_copy(
        src_ref=source,
        dst_ref=target,
        send_sem=send_sem,
        recv_sem=recv_sem,
        device_id={axis: peer},
        device_id_type=MESH,
    )


def spread(me, source, target, sems, peers):
    send, recv = sems
    for peer in peers:

        @pl.when(peer != me)
        def _(peer=peer):
            remote(source.at[peer], target.at[me], send.at[peer], recv.at[me], peer).start()


def team_peers(me, team):
    return [team * 8 + lax.rem(me + n, 8) for n in range(8)]


def settle(me, source, target, sems):
    send, recv = sems
    for hop in range(1, SEQ):
        peer = lax.rem(me + hop, SEQ)
        remote(source.at[peer], target.at[peer], send.at[peer], recv.at[peer], peer).wait()


def share(me, source, target, sems):
    send, recv = sems
    for hop in range(1, SEQ):
        peer = lax.rem(me + hop, SEQ)
        remote(source, target.at[me], send.at[peer], recv.at[me], peer).start()


def settle_share(me, source, target, sems):
    send, recv = sems
    for hop in range(1, SEQ):
        peer = lax.rem(me + hop, SEQ)
        remote(source, target.at[peer], send.at[peer], recv.at[peer], peer).wait()


def lanes(head):
    return pl.ds(pl.multiple_of(head * HEAD, HEAD), HEAD)


PAIR = 2


def whole_kernel(
    lens_ref, bias_ref, q_ref, k_ref, v_ref, qm_ref, km_ref, bw_ref, proj_ref,
    dq_ref, dk_ref, row_ref, loss_out,
    zq_ref, zk_ref, beta_ref, t_ref, w_ref, sc_ref, qe_ref, grad_ref,
    loss_ref, gap_ref, s_ref, hops_ref,
    pa_ref, got, s_in, keys_at, values_at,
    ds_ref, ds_got, outs, lam_ref, pq, pq_got, pq_own, pq_all, pk, pk_got, pk_own, pk_all,
    w, sib_out, sib_in, far, up, down, in_a, in_b, in_up, in_down, r,
    w_sem, sib_send, sib_recv, rs_send, rs_recv, ag_send, ag_recv,
    kv_send, kv_recv, front_send1, front_recv1, front_send2, front_recv2,
    send1, recv1, send2, recv2, send3, recv3, send4, recv4, send5, recv5, send6, recv6,
    send7, recv7, send8, recv8,
):
    me = lax.axis_index("seq")
    head = lax.axis_index("head")
    z, core = head // 2, lax.rem(head, 2)
    zp, zm, z2 = lax.rem(z + 1, 4), lax.rem(z + 3, 4), lax.rem(z + 2, 4)
    above, below, sibling = zp * 2 + core, zm * 2 + core, z * 2 + (1 - core)
    order = (z2, zp, zm, z)

    def weight_copy(side, quarter, half):
        at = side * 8 + quarter * 2 + half
        return pltpu.make_async_copy(
            proj_ref.at[:, pl.ds(pl.multiple_of(at * HALF, HALF), HALF)], w.at[at], w_sem.at[at]
        )

    first = me * ROWS
    k = k_ref[...]
    v16 = v_ref[...]
    v = v16.astype(f32)
    x, y = me // 4, lax.rem(me, 4)
    xp, xm, yp, ym = lax.rem(x + 1, 4), lax.rem(x + 3, 4), lax.rem(y + 1, 4), lax.rem(y + 3, 4)
    keys_at[x, y] = k
    values_at[y, x] = v16
    for side in (1 - core, core):
        for quarter in order:
            for half in range(2):
                weight_copy(side, quarter, half).start()
    signal_all([("head", above), ("head", below), ("head", sibling)] + seq_peers(me))

    def relay(n, source, peer):
        return remote(source, source, kv_send.at[n], kv_recv.at[n], peer)

    across = []
    for d in range(1, 4):
        across.append(relay(d - 1, keys_at.at[x, y], x * 4 + lax.rem(y + d, 4)))
        across.append(relay(d + 2, values_at.at[y, x], lax.rem(x + d, 4) * 4 + y))
    whole_rows = [
        relay(6, keys_at.at[x], xp * 4 + y),
        relay(7, keys_at.at[x], xm * 4 + y),
        relay(8, values_at.at[y], x * 4 + yp),
        relay(9, values_at.at[y], x * 4 + ym),
    ]
    far_rows = [
        relay(10, keys_at.at[xm, pl.ds(0, 2)], xp * 4 + y),
        relay(11, keys_at.at[xp, pl.ds(2, 2)], xm * 4 + y),
        relay(12, values_at.at[ym, pl.ds(0, 2)], x * 4 + yp),
        relay(13, values_at.at[yp, pl.ds(2, 2)], x * 4 + ym),
    ]
    for copy in across:
        copy.start()

    def pass_on(turn):
        @pl.when(turn == 0)
        def _():
            for copy in across:
                copy.wait_recv()
            for copy in whole_rows:
                copy.start()

        @pl.when(turn == 1)
        def _():
            for copy in whole_rows:
                copy.wait_recv()
            for copy in far_rows:
                copy.start()

    start = row_starts(lens_ref, first)
    lead = (start < 0).astype(f32)
    lead_last = lead[ROWS - 1 :, :]
    tail = (start == start[ROWS - 1 :, :]).astype(f32)
    ri, ci = iotas()
    allowed = (ci <= ri) & (ci >= start)
    strict = (ci < ri) & (ci >= start)
    team = range(TEAM)

    def prepare(turn, _):
        heads = [turn * TEAM + n for n in team]
        qus, kus, betas = [], [], []
        for h in heads:
            q = q_ref[:, lanes(h)]
            qh, ql = split(qm_ref[h])
            kh, kl = split(km_ref[h])
            zq = mm(q, qh, NN) + mm(q, ql, NN)
            zk = mm(k, kh, NN) + mm(k, kl, NN)
            zq_ref[h] = zq
            zk_ref[h] = zk
            logits = jnp.sum(q.astype(f32) * bw_ref[h], axis=-1, keepdims=True)
            beta = sigmoid(logits + bias_ref[h])
            beta_ref[h] = beta
            qus.append(unit(zq))
            kus.append(unit(zk))
            betas.append(beta)
        lows = [jnp.where(strict, betas[n] * d3(kus[n], kus[n], NT), 0.0) for n in team]
        invs = lower_inverses(lows, ri, ci)
        pass_on(turn)
        ws = [
            d3(invs[n], jnp.concatenate([betas[n] * kus[n], betas[n] * v], axis=1), NN)
            for n in team
        ]
        scores = [jnp.where(allowed, d3(qus[n], kus[n], NT), 0.0) for n in team]
        for n, h in enumerate(heads):
            t_ref[h] = invs[n]
            w_ref[h] = ws[n]
            sc_ref[h] = scores[n]
            mixed = d3(scores[n], ws[n], NN)
            qe_ref[h] = qus[n] - mixed[:, :HEAD]
            grad_ref[:, lanes(h)] = mixed[:, HEAD:]
            both = jnp.concatenate([ws[n][:, :HEAD], tail * ws[n][:, HEAD:]], axis=1)
            pair = d3(both, kus[n], TN)
            hop = (-lead_last * pair[:HEAD]).astype(bf16)
            add = pair[HEAD:].astype(bf16)
            for side in range(2):
                pa_ref[2 * h + side, :HEAD] = hop
                pa_ref[2 * h + side, HEAD:] = add[side * (HEAD // 2) : (side + 1) * (HEAD // 2)]
        spread(me, pa_ref, got, (front_send1, front_recv1), team_peers(me, turn))
        return _

    lax.fori_loop(0, HEADS // TEAM, prepare, 0)
    for copy in far_rows:
        copy.wait_recv()
    scale = math.log2(math.e) / math.sqrt(HEAD)
    row = lax.broadcasted_iota(jnp.int32, (ROWS, 1), 0)
    lane = lax.broadcasted_iota(jnp.int32, (1, KEY_BLOCK), 1)

    def attend(turn, _):
        queries = []
        for n in range(PAIR):
            hi, lo = split(q_ref[:, lanes(turn * PAIR + n)].astype(f32) * scale)
            queries.append(jnp.concatenate([hi, lo], axis=1))

        def step(block, carry):
            keys = keys_at[pl.ds(2 * block, 2)].reshape(KEY_BLOCK, HEAD)
            keys = jnp.concatenate([keys, keys], axis=1)
            values = jnp.concatenate(
                [values_at[n, 2 * block + at] for at in range(2) for n in range(4)], axis=0
            )
            values = jnp.concatenate([values, jnp.ones((KEY_BLOCK, HEAD), bf16)], axis=1)
            u = lane + (block * KEY_BLOCK - first)
            seen = (u >= start) & (u <= row)
            out = []
            for query, (peak, acc) in zip(queries, carry):
                s = jnp.where(seen, mm(query, keys, NT), -1e30)
                new = jnp.maximum(peak, jnp.max(s, axis=-1, keepdims=True))
                weights = jnp.exp2(s - new).astype(bf16)
                out.append((new, acc * jnp.exp2(peak - new) + mm(weights, values, NN)))
            return tuple(out)

        carry = tuple(
            (jnp.full((ROWS, 1), -1e30, f32), jnp.zeros((ROWS, 2 * HEAD), f32))
            for _ in range(PAIR)
        )
        carry = lax.fori_loop(0, (first + ROWS - 1) // KEY_BLOCK + 1, step, carry)
        for n in range(PAIR):
            acc = carry[n][1]
            grad_ref[:, lanes(turn * PAIR + n)] -= acc[:, :HEAD] / acc[:, HEAD : HEAD + 1]
        return _

    lax.fori_loop(0, 2, attend, 0)
    got[me] = pa_ref[me]
    settle(me, pa_ref, got, (front_send1, front_recv1))

    keeps = [kept(lens_ref, i) for i in range(SEQ)]
    state = jnp.zeros((HEAD // 2, HEAD), f32)
    for i in range(SEQ):
        outs[i] = state.astype(bf16)
        block = got[i]
        hops_ref[i] = block[:HEAD]
        hop = block[:HEAD]
        state = keeps[i] * state + d2(state, hop, NN) + block[HEAD:].astype(f32)
    for turn in range(2):
        spread(me, outs, s_in, (front_send2, front_recv2), team_peers(me, turn))
    s_in[me] = outs[me]
    lax.fori_loop(2, 4, attend, 0)
    settle(me, outs, s_in, (front_send2, front_recv2))
    for h in range(HEADS):
        state = jnp.concatenate([s_in[2 * h], s_in[2 * h + 1]], axis=0)
        s_ref[h] = state
        gap = lead * d3(qe_ref[h], state, NT) + grad_ref[:, h * HEAD : (h + 1) * HEAD]
        gap_ref[:, h * HEAD : (h + 1) * HEAD] = gap.astype(bf16)
    for copy in across + whole_rows + far_rows:
        copy.wait_send()

    def send(source, target, peer, send_sem, recv_sem):
        copy = remote(source, target, send_sem, recv_sem, peer, "head")
        copy.start()
        return copy

    gap = gap_ref[...]

    def part(side, quarter, half):
        weight_copy(side, quarter, half).wait()
        return mm(gap, w[side * 8 + quarter * 2 + half], NN)

    sib = []
    for n, quarter in enumerate(order):
        for half in range(2):
            sib_out[n, half] = part(1 - core, quarter, half).astype(bf16)
        sib.append(send(sib_out.at[n], sib_in.at[n], sibling, sib_send.at[n], sib_recv.at[n]))

    def pair(n, half):
        return part(core, order[n], half) + sib_in[n, half].astype(f32)

    sib[0].wait_recv()
    far[0] = pair(0, 0).astype(bf16)
    send_a = send(far.at[0], in_a, above, rs_send.at[0], rs_recv.at[0])
    far[1] = pair(0, 1).astype(bf16)
    send_b = send(far.at[1], in_b, below, rs_send.at[1], rs_recv.at[1])
    sib[1].wait_recv()
    up[1] = pair(1, 1).astype(bf16)
    first_up = pair(1, 0)
    send_a.wait_recv()
    up[0] = (first_up + in_a[...].astype(f32)).astype(bf16)
    send_up = send(up, in_up, above, rs_send.at[2], rs_recv.at[2])
    sib[2].wait_recv()
    down[0] = pair(2, 0).astype(bf16)
    first_down = pair(2, 1)
    send_b.wait_recv()
    down[1] = (first_down + in_b[...].astype(f32)).astype(bf16)
    send_down = send(down, in_down, below, rs_send.at[3], rs_recv.at[3])
    sib[3].wait_recv()
    mine = [pair(3, 0), pair(3, 1)]
    send_up.wait_recv()
    send_down.wait_recv()
    own = core * 4 + z
    for half in range(2):
        total = mine[half] + (in_up[half].astype(f32) + in_down[half].astype(f32))
        r[own, half] = total.astype(bf16)

    def gather(chunk, half, peer, n):
        ref = r.at[chunk] if half is None else r.at[chunk, half]
        return send(ref, ref, peer, ag_send.at[n], ag_recv.at[n])

    loss_ref[...] = jnp.zeros_like(loss_ref)

    def use(chunk, half, first=False):
        block = r[chunk, half]
        term = 2.0 * mm(block, w[chunk * 2 + half], NT)
        grad_ref[...] = term if first else grad_ref[...] + term
        wide = block.astype(f32)
        loss_ref[...] += jnp.sum(wide * wide, axis=0, keepdims=True)

    sides = core * 4
    others = (1 - core) * 4
    own_up = gather(own, None, above, 0)
    own_down = gather(own, None, below, 1)
    own_sib = gather(own, None, sibling, 2)
    use(own, 0, True)
    use(own, 1)
    own_sib.wait_recv()
    use(others + z, 0)
    use(others + z, 1)
    own_up.wait_recv()
    pass_a = gather(sides + zm, 0, above, 3)
    sib_m = gather(sides + zm, None, sibling, 4)
    own_down.wait_recv()
    pass_b = gather(sides + zp, 1, below, 5)
    sib_p = gather(sides + zp, None, sibling, 6)
    use(sides + zm, 0)
    use(sides + zm, 1)
    use(sides + zp, 0)
    use(sides + zp, 1)
    sib_m.wait_recv()
    use(others + zm, 0)
    use(others + zm, 1)
    sib_p.wait_recv()
    use(others + zp, 0)
    use(others + zp, 1)
    pass_a.wait_recv()
    sib_a = gather(sides + z2, 0, sibling, 7)
    pass_b.wait_recv()
    sib_b = gather(sides + z2, 1, sibling, 8)
    use(sides + z2, 0)
    use(sides + z2, 1)
    sib_a.wait_recv()
    use(others + z2, 0)
    sib_b.wait_recv()
    use(others + z2, 1)
    for copy in sib + [
        send_a, send_b, send_up, send_down, own_up, own_down, own_sib,
        pass_a, sib_m, pass_b, sib_p, sib_a, sib_b,
    ]:
        copy.wait_send()
    half = HEAD // 2

    def state_grads(turn, _):
        for n in team:
            h = turn * TEAM + n
            ds = d3(lead * grad_ref[:, lanes(h)], qe_ref[h], TN).astype(bf16)
            ds_ref[2 * h] = ds[:half]
            ds_ref[2 * h + 1] = ds[half:]
        spread(me, ds_ref, ds_got, (send1, recv1), team_peers(me, turn))
        return _

    lax.fori_loop(0, HEADS // TEAM, state_grads, 0)

    def query_side(turn, _):
        heads = [turn * TEAM + n for n in team]
        gs = [grad_ref[:, lanes(h)] for h in heads]
        dqes = [d3(lead * g, s_ref[h], NN) for h, g in zip(heads, gs)]
        boths = [jnp.concatenate([-dqe, g], axis=1) for dqe, g in zip(dqes, gs)]
        dscs = [jnp.where(allowed, d3(b, w_ref[h], NT), 0.0) for h, b in zip(heads, boths)]
        for h, both in zip(heads, boths):
            sc_ref[h] = d3(sc_ref[h], both, TN)
        for n, h in enumerate(heads):
            zq = zq_ref[h]
            qe_ref[h] = d3(dscs[n], unit(zq), TN)
            dqu = dqes[n] + d3(dscs[n], unit(zk_ref[h]), NN)
            dqm = d2r(q_ref[:, lanes(h)], unit_back(zq, dqu), TN)
            pq[2 * h] = dqm[:half]
            pq[2 * h + 1] = dqm[half:]
        return _

    query_side(0, 0)
    ds_got[me] = ds_ref[me]
    settle(me, ds_ref, ds_got, (send1, recv1))

    keeps = [kept(lens_ref, i) for i in range(SEQ)]
    state = jnp.zeros((half, HEAD), f32)
    for i in reversed(range(SEQ)):
        outs[i] = state.astype(bf16)
        state = keeps[i] * state + d2(state, hops_ref[i], NT) + ds_got[i].astype(f32)
    for turn in range(2):
        spread(me, outs, lam_ref, (send2, recv2), team_peers(me, turn))
    lam_ref[me] = outs[me]
    query_side(1, 0)
    spread(me, pq, pq_got, (send3, recv3), [p for _, p in seq_peers(me)])

    settle(me, outs, lam_ref, (send2, recv2))

    loss = jnp.broadcast_to(jnp.sum(loss_ref[...], axis=1, keepdims=True), (1, HEAD))

    key_sems = [(send5, recv5), (send7, recv7)]
    share_sems = [(send6, recv6), (send8, recv8)]

    def key_total(turn):
        pk_got[turn, me] = pk[turn, me]
        settle(me, pk.at[turn], pk_got.at[turn], key_sems[turn])
        total = pk_got[turn, 0]
        for i in range(1, SEQ):
            total = total + pk_got[turn, i]
        pk_own[turn] = total[:32].astype(bf16)
        row_ref[turn * TEAM : (turn + 1) * TEAM] = total[32:36]
        share(me, pk_own.at[turn], pk_all.at[turn], share_sems[turn])
        pk_all[turn, me] = pk_own[turn]
        return total

    def key_side(turn):
        heads = [turn * TEAM + n for n in team]
        lams = [jnp.concatenate([lam_ref[2 * h], lam_ref[2 * h + 1]], axis=0) for h in heads]
        kus = [unit(zk_ref[h]) for h in heads]
        ws = [w_ref[h] for h in heads]
        dhops = [lead_last * mm(s_ref[h], lams[n], TN) for n, h in enumerate(heads)]
        drs = []
        for n, h in enumerate(heads):
            dwk = sc_ref[h, :, :HEAD] - d3(kus[n], dhops[n], NT)
            dwv = sc_ref[h, :, HEAD:] + tail * d2(kus[n], lams[n], NT)
            drs.append(d3(t_ref[h], jnp.concatenate([dwk, dwv], axis=1), TN))
        dkus = [
            qe_ref[h]
            - d3(ws[n][:, :HEAD], dhops[n], NN)
            + tail * d2(ws[n][:, HEAD:], lams[n], NN)
            for n, h in enumerate(heads)
        ]
        dlows = [jnp.where(strict, -d3(drs[n], ws[n], NT), 0.0) for n in team]
        kterms = [drs[n][:, :HEAD] + d3(dlows[n], kus[n], NN) for n in team]
        dkm_rows, extra = [], []
        for n, h in enumerate(heads):
            beta = beta_ref[h]
            dbeta = jnp.sum(kterms[n] * kus[n] + drs[n][:, HEAD:] * v, axis=-1, keepdims=True)
            dku = dkus[n] + beta * kterms[n] + d3(beta * dlows[n], kus[n], TN)
            dkm = d2r(k, unit_back(zk_ref[h], dku), TN)
            dlogit = dbeta * beta * (1.0 - beta)
            q = q_ref[:, lanes(h)].astype(f32)
            dkm_rows.append(dkm.reshape(SEQ, 8, HEAD))
            extra.append(jnp.sum(q * dlogit, axis=0, keepdims=True))
        extra = jnp.concatenate(extra + [loss, jnp.zeros((3, HEAD), f32)], axis=0)
        pk[turn, :, :32] = jnp.concatenate(dkm_rows, axis=1)
        pk[turn, :, 32:] = jnp.broadcast_to(extra[None], (SEQ, 8, HEAD))
        spread(me, pk.at[turn], pk_got.at[turn], key_sems[turn], [p for _, p in seq_peers(me)])

    key_side(0)
    pq_got[me] = pq[me]
    settle(me, pq, pq_got, (send3, recv3))
    pq_own[...] = lax.fori_loop(
        0, SEQ, lambda i, total: total + pq_got[i], jnp.zeros((half, HEAD), f32)
    ).astype(bf16)
    share(me, pq_own, pq_all, (send4, recv4))
    pq_all[me] = pq_own[...]
    key_side(1)
    key_total(0)
    total = key_total(1)
    loss_out[...] = total[36:37]
    settle_share(me, pq_own, pq_all, (send4, recv4))
    dq_ref[...] = pq_all[...]
    for turn in range(2):
        settle_share(me, pk_own.at[turn], pk_all.at[turn], share_sems[turn])
    dk_ref[...] = pk_all[...]


def finish_kernel(dq_in, dk_in, row_in, loss_in, dq_ref, dk_ref, row_ref, loss_ref):
    dq_ref[...] = dq_in[...].astype(f32)
    for turn in range(HEADS // TEAM):
        wide = dk_in[turn].astype(f32)
        for n in range(TEAM):
            dk_ref[turn * TEAM + n] = wide[:, n * 8 : (n + 1) * 8].reshape(HEAD, HEAD)
    row_ref[...] = row_in[...]
    loss_ref[...] = loss_in[:, :1] / (SEQ * ROWS * WIDTH)


def shape(dims, dtype):
    return jax.ShapeDtypeStruct(dims, dtype)


SMEM = pl.BlockSpec(memory_space=pltpu.SMEM)
VMEM = pl.BlockSpec(memory_space=pltpu.VMEM)
ANY = pl.BlockSpec(memory_space=pl.ANY)


def params(**more):
    return pltpu.CompilerParams(vmem_limit_bytes=VMEM_BYTES, has_side_effects=True, **more)


def shards(q, k, v, lens, proj, query_map, key_map, beta_weight, beta_bias):
    bw = beta_weight.reshape(HEADS, 1, HEAD)
    square = (HEADS, ROWS, ROWS)
    slab = (HEADS, ROWS, HEAD)
    halves = (SEQ, HEAD // 2, HEAD)
    extended = (2, SEQ, 40, HEAD)
    shares = (2, SEQ, 32, HEAD)
    block = (2, ROWS, HALF)
    scratch = [
        (slab, f32), (slab, f32), ((HEADS, ROWS, 1), f32), (square, f32), (square, f32),
        (square, f32), (slab, f32), ((ROWS, HEADS * HEAD), f32),
        ((1, HALF), f32), ((ROWS, HEADS * HEAD), bf16), ((HEADS, HEAD, HEAD), bf16),
        ((SEQ, HEAD, HEAD), bf16),
        ((SEQ, 192, HEAD), bf16), ((SEQ, 192, HEAD), bf16), (halves, bf16),
        ((4, 4, ROWS, HEAD), bf16), ((4, 4, ROWS, HEAD), bf16),
        (halves, bf16), (halves, bf16), (halves, bf16), (halves, bf16),
        (halves, f32), (halves, f32), (halves[1:], bf16), (halves, bf16),
        (extended, f32), (extended, f32), ((2, 32, HEAD), bf16), (shares, bf16),
        ((16, HEADS * HEAD, HALF), bf16), ((4,) + block, bf16), ((4,) + block, bf16),
        (block, bf16), (block, bf16), (block, bf16), (block[1:], bf16), (block[1:], bf16),
        (block, bf16), (block, bf16), ((8,) + block, bf16),
    ]
    sems = [16, 4, 4, 4, 4, 9, 9] + [SEQ] * 22
    partial = pl.pallas_call(
        whole_kernel,
        in_specs=[SMEM, SMEM] + [VMEM] * 6 + [ANY],
        out_specs=[VMEM] * 4,
        out_shape=[
            shape(halves, bf16), shape(shares, bf16), shape((HEADS, HEAD), f32),
            shape((1, HEAD), f32),
        ],
        scratch_shapes=[pltpu.VMEM(dims, kind) for dims, kind in scratch]
        + [pltpu.SemaphoreType.DMA((count,)) for count in sems],
        compiler_params=params(collective_id=0),
        name="whole",
    )(lens, beta_bias, q, k, v, query_map, key_map, bw, proj)
    grad_query, grad_key, grad_beta, loss = pl.pallas_call(
        finish_kernel,
        in_specs=[VMEM] * 4,
        out_specs=[VMEM] * 4,
        out_shape=[
            shape(halves, f32), shape((HEADS, HEAD, HEAD), f32), shape((HEADS, HEAD), f32),
            shape((1, 1), f32),
        ],
        name="finish",
    )(*partial)
    return loss.reshape(()), grad_query.reshape(HEADS, HEAD, HEAD), grad_key, grad_beta


def solution(mesh):
    return jax.shard_map(
        shards,
        mesh=mesh,
        in_specs=(
            P("seq", "head"),
            P("seq", "head"),
            P("seq", "head"),
            P(),
            P("head", None),
            P("head", None, None),
            P("head", None, None),
            P("head", None),
            P("head"),
        ),
        out_specs=(P(), P("head", None, None), P("head", None, None), P("head", None)),
        check_vma=False,
    )
```

```python
import functools
import math

import jax
import jax.numpy as jnp
from jax import lax
from jax.experimental import pallas as pl
from jax.experimental.pallas import tpu as pltpu
from jax.sharding import PartitionSpec as P

HEAD = 128
ROWS = 256
HEADS = 8
SEQ = 16
NDOCS = 8
WIDTH = 8192
HALF = 512
KEY_BLOCK = 2048
TEAM = 4

f32 = jnp.float32
bf16 = jnp.bfloat16
NN = ((1,), (0,))
NT = ((1,), (1,))
TN = ((0,), (0,))
VMEM_BYTES = 62 * 1024 * 1024
MESH = pl.DeviceIdType.MESH


def mm(a, b, dims):
    return lax.dot_general(a, b, (dims, ((), ())), preferred_element_type=f32)


def split(x):
    hi = x.astype(bf16)
    return hi, (x - hi.astype(f32)).astype(bf16)


def d1(a, b, dims):
    return mm(a.astype(bf16), b.astype(bf16), dims)


def d3(a, b, dims):
    ah, al = split(a)
    bh, bl = split(b)
    return mm(ah, bh, dims) + (mm(ah, bl, dims) + mm(al, bh, dims))


def d2(a, b, dims):
    ah, al = split(a)
    return mm(ah, b, dims) + mm(al, b, dims)


def d2r(a, b, dims):
    bh, bl = split(b)
    return mm(a, bh, dims) + mm(a, bl, dims)


def row_starts(lens_ref, first_row):
    t = lax.broadcasted_iota(jnp.int32, (ROWS, 1), 0) + first_row
    start = jnp.zeros((ROWS, 1), jnp.int32)
    at = jnp.int32(0)
    for doc in range(NDOCS):
        start = jnp.where(t >= at, at, start)
        at = at + lens_ref[doc]
    return start - first_row


def iotas():
    return (
        lax.broadcasted_iota(jnp.int32, (ROWS, ROWS), 0),
        lax.broadcasted_iota(jnp.int32, (ROWS, ROWS), 1),
    )


def sigmoid(z):
    return 1.0 / (1.0 + jnp.exp(-z))


def unit(z):
    act = z * sigmoid(z)
    scale = lax.rsqrt(jnp.sum(act * act, axis=-1, keepdims=True) + 1e-06)
    return act * scale


def unit_back(z, grad):
    gate = sigmoid(z)
    act = z * gate
    scale = lax.rsqrt(jnp.sum(act * act, axis=-1, keepdims=True) + 1e-06)
    out = act * scale
    act_grad = scale * (grad - out * jnp.sum(out * grad, axis=-1, keepdims=True))
    return act_grad * (gate * (1.0 + z * (1.0 - gate)))


def lower_inverses(lows, ri, ci):
    half = ROWS // 2
    eye = (ri == ci).astype(f32)
    r, c = ri[:half, :half], ci[:half, :half]
    parts = [p for low in lows for p in (low[:half, :half], low[half:, half:])]
    small = eye[:half, :half]
    near = (r >> 1) == (c >> 1)
    invs = [small - jnp.where(near, p, 0.0) for p in parts]
    parts = [p.astype(bf16) for p in parts]
    for k in range(1, 7):
        ring = ((r >> (k + 1)) == (c >> (k + 1))) & ((r >> k) != (c >> k))
        inv16 = [inv.astype(bf16) for inv in invs]
        mids = [
            mm(jnp.where(ring, p, jnp.zeros_like(p)), i, NN).astype(bf16)
            for p, i in zip(parts, inv16)
        ]
        invs = [inv - mm(i, mid, NN) for inv, i, mid in zip(invs, inv16, mids)]
    whole = []
    for n, low in enumerate(lows):
        top, bottom = invs[2 * n], invs[2 * n + 1]
        corner = -d1(d1(bottom, low[half:, :half], NN), top, NN)
        upper = jnp.concatenate([top, jnp.zeros((half, half), f32)], axis=1)
        lower = jnp.concatenate([corner, bottom], axis=1)
        whole.append(jnp.concatenate([upper, lower], axis=0))
    misses = [(eye - inv) - d3(low, inv, NN) for low, inv in zip(lows, whole)]
    return [inv + d1(inv, miss, NN) for inv, miss in zip(whole, misses)]


def kept(lens_ref, i):
    start = jnp.int32(0)
    at = jnp.int32(0)
    for doc in range(NDOCS):
        start = jnp.where((i + 1) * ROWS > at, at, start)
        at = at + lens_ref[doc]
    return jnp.where(start < i * ROWS, 1.0, 0.0).astype(f32)


def signal_all(peers):
    barrier = pltpu.get_barrier_semaphore()
    for axis, index in peers:
        pl.semaphore_signal(barrier, inc=1, device_id={axis: index}, device_id_type=MESH)
    pl.semaphore_wait(barrier, len(peers))


def seq_peers(me):
    return [("seq", lax.rem(me + hop, SEQ)) for hop in range(1, SEQ)]


def remote(source, target, send_sem, recv_sem, peer, axis="seq"):
    return pltpu.make_async_remote_copy(
        src_ref=source,
        dst_ref=target,
        send_sem=send_sem,
        recv_sem=recv_sem,
        device_id={axis: peer},
        device_id_type=MESH,
    )


def spread(me, source, target, sems, peers):
    send, recv = sems
    for peer in peers:

        @pl.when(peer != me)
        def _(peer=peer):
            remote(source.at[peer], target.at[me], send.at[peer], recv.at[me], peer).start()


def team_peers(me, team):
    return [team * 8 + lax.rem(me + n, 8) for n in range(8)]


def settle(me, source, target, sems):
    send, recv = sems
    for hop in range(1, SEQ):
        peer = lax.rem(me + hop, SEQ)
        remote(source.at[peer], target.at[peer], send.at[peer], recv.at[peer], peer).wait()


def share(me, source, target, sems):
    send, recv = sems
    for hop in range(1, SEQ):
        peer = lax.rem(me + hop, SEQ)
        remote(source, target.at[me], send.at[peer], recv.at[me], peer).start()


def settle_share(me, source, target, sems):
    send, recv = sems
    for hop in range(1, SEQ):
        peer = lax.rem(me + hop, SEQ)
        remote(source, target.at[peer], send.at[peer], recv.at[peer], peer).wait()


def lanes(head):
    return pl.ds(pl.multiple_of(head * HEAD, HEAD), HEAD)


PAIR = 2


def whole_kernel(
    lens_ref, bias_ref, q_ref, k_ref, v_ref, qm_ref, km_ref, bw_ref, proj_ref,
    dq_ref, dk_ref, row_ref, loss_out,
    zq_ref, zk_ref, beta_ref, t_ref, w_ref, sc_ref, qe_ref, grad_ref,
    loss_ref, gap_ref, s_ref, hops_ref,
    pa_ref, got, s_in, keys_at, values_at,
    ds_ref, ds_got, outs, lam_ref, pq, pq_got, pq_own, pq_all, pk, pk_got, pk_own, pk_all,
    w, sib_out, sib_in, far, up, down, in_a, in_b, in_up, in_down, r,
    w_sem, sib_send, sib_recv, rs_send, rs_recv, ag_send, ag_recv,
    kv_send, kv_recv, front_send1, front_recv1, front_send2, front_recv2,
    send1, recv1, send2, recv2, send3, recv3, send4, recv4, send5, recv5, send6, recv6,
    send7, recv7, send8, recv8,
):
    me = lax.axis_index("seq")
    head = lax.axis_index("head")
    z, core = head // 2, lax.rem(head, 2)
    zp, zm, z2 = lax.rem(z + 1, 4), lax.rem(z + 3, 4), lax.rem(z + 2, 4)
    above, below, sibling = zp * 2 + core, zm * 2 + core, z * 2 + (1 - core)
    order = (z2, zp, zm, z)

    def weight_copy(side, quarter, half):
        at = side * 8 + quarter * 2 + half
        return pltpu.make_async_copy(
            proj_ref.at[:, pl.ds(pl.multiple_of(at * HALF, HALF), HALF)], w.at[at], w_sem.at[at]
        )

    first = me * ROWS
    k = k_ref[...]
    v16 = v_ref[...]
    v = v16.astype(f32)
    x, y = me // 4, lax.rem(me, 4)
    xp, xm, yp, ym = lax.rem(x + 1, 4), lax.rem(x + 3, 4), lax.rem(y + 1, 4), lax.rem(y + 3, 4)
    keys_at[x, y] = k
    values_at[y, x] = v16
    for side in (1 - core, core):
        for quarter in order:
            for half in range(2):
                weight_copy(side, quarter, half).start()
    signal_all([("head", above), ("head", below), ("head", sibling)] + seq_peers(me))

    def relay(n, source, peer):
        return remote(source, source, kv_send.at[n], kv_recv.at[n], peer)

    across = []
    for d in range(1, 4):
        across.append(relay(d - 1, keys_at.at[x, y], x * 4 + lax.rem(y + d, 4)))
        across.append(relay(d + 2, values_at.at[y, x], lax.rem(x + d, 4) * 4 + y))
    whole_rows = [
        relay(6, keys_at.at[x], xp * 4 + y),
        relay(7, keys_at.at[x], xm * 4 + y),
        relay(8, values_at.at[y], x * 4 + yp),
        relay(9, values_at.at[y], x * 4 + ym),
    ]
    far_rows = [
        relay(10, keys_at.at[xm, pl.ds(0, 2)], xp * 4 + y),
        relay(11, keys_at.at[xp, pl.ds(2, 2)], xm * 4 + y),
        relay(12, values_at.at[ym, pl.ds(0, 2)], x * 4 + yp),
        relay(13, values_at.at[yp, pl.ds(2, 2)], x * 4 + ym),
    ]
    for copy in across:
        copy.start()

    def pass_on(turn):
        @pl.when(turn == 0)
        def _():
            for copy in across:
                copy.wait_recv()
            for copy in whole_rows:
                copy.start()

        @pl.when(turn == 1)
        def _():
            for copy in whole_rows:
                copy.wait_recv()
            for copy in far_rows:
                copy.start()

    start = row_starts(lens_ref, first)
    lead = (start < 0).astype(f32)
    lead_last = lead[ROWS - 1 :, :]
    tail = (start == start[ROWS - 1 :, :]).astype(f32)
    ri, ci = iotas()
    allowed = (ci <= ri) & (ci >= start)
    strict = (ci < ri) & (ci >= start)
    team = range(TEAM)

    def prepare(turn, _):
        heads = [turn * TEAM + n for n in team]
        qus, kus, betas = [], [], []
        for h in heads:
            q = q_ref[:, lanes(h)]
            qh, ql = split(qm_ref[h])
            kh, kl = split(km_ref[h])
            zq = mm(q, qh, NN) + mm(q, ql, NN)
            zk = mm(k, kh, NN) + mm(k, kl, NN)
            zq_ref[h] = zq
            zk_ref[h] = zk
            logits = jnp.sum(q.astype(f32) * bw_ref[h], axis=-1, keepdims=True)
            beta = sigmoid(logits + bias_ref[h])
            beta_ref[h] = beta
            qus.append(unit(zq))
            kus.append(unit(zk))
            betas.append(beta)
        lows = [jnp.where(strict, betas[n] * d3(kus[n], kus[n], NT), 0.0) for n in team]
        invs = lower_inverses(lows, ri, ci)
        pass_on(turn)
        ws = [
            d3(invs[n], jnp.concatenate([betas[n] * kus[n], betas[n] * v], axis=1), NN)
            for n in team
        ]
        scores = [jnp.where(allowed, d3(qus[n], kus[n], NT), 0.0) for n in team]
        for n, h in enumerate(heads):
            t_ref[h] = invs[n]
            w_ref[h] = ws[n]
            sc_ref[h] = scores[n]
            mixed = d3(scores[n], ws[n], NN)
            qe_ref[h] = qus[n] - mixed[:, :HEAD]
            grad_ref[:, lanes(h)] = mixed[:, HEAD:]
            both = jnp.concatenate([ws[n][:, :HEAD], tail * ws[n][:, HEAD:]], axis=1)
            pair = d3(both, kus[n], TN)
            hop = (-lead_last * pair[:HEAD]).astype(bf16)
            add = pair[HEAD:].astype(bf16)
            for side in range(2):
                pa_ref[2 * h + side, :HEAD] = hop
                pa_ref[2 * h + side, HEAD:] = add[side * (HEAD // 2) : (side + 1) * (HEAD // 2)]
        spread(me, pa_ref, got, (front_send1, front_recv1), team_peers(me, turn))
        return _

    lax.fori_loop(0, HEADS // TEAM, prepare, 0)
    for copy in far_rows:
        copy.wait_recv()
    scale = math.log2(math.e) / math.sqrt(HEAD)
    row = lax.broadcasted_iota(jnp.int32, (ROWS, 1), 0)
    lane = lax.broadcasted_iota(jnp.int32, (1, KEY_BLOCK), 1)

    def attend(turn, _):
        queries = []
        for n in range(PAIR):
            hi, lo = split(q_ref[:, lanes(turn * PAIR + n)].astype(f32) * scale)
            queries.append(jnp.concatenate([hi, lo], axis=1))
        query = jnp.concatenate(queries, axis=0)

        def step(block, carry):
            keys = keys_at[pl.ds(2 * block, 2)].reshape(KEY_BLOCK, HEAD)
            keys = jnp.concatenate([keys, keys], axis=1)
            values = jnp.concatenate(
                [values_at[n, 2 * block + at] for at in range(2) for n in range(4)], axis=0
            )
            values = jnp.concatenate([values, jnp.ones((KEY_BLOCK, HEAD), bf16)], axis=1)
            u = lane + (block * KEY_BLOCK - first)
            seen = (u >= start) & (u <= row)
            scores = mm(query, keys, NT)
            out = []
            for n, (peak, acc) in enumerate(carry):
                s = jnp.where(seen, scores[n * ROWS : (n + 1) * ROWS], -1e30)
                new = jnp.maximum(peak, jnp.max(s, axis=-1, keepdims=True))
                weights = jnp.exp2(s - new).astype(bf16)
                out.append((new, acc * jnp.exp2(peak - new) + mm(weights, values, NN)))
            return tuple(out)

        carry = tuple(
            (jnp.full((ROWS, 1), -1e30, f32), jnp.zeros((ROWS, 2 * HEAD), f32))
            for _ in range(PAIR)
        )
        carry = lax.fori_loop(0, (first + ROWS - 1) // KEY_BLOCK + 1, step, carry)
        for n in range(PAIR):
            acc = carry[n][1]
            grad_ref[:, lanes(turn * PAIR + n)] -= acc[:, :HEAD] / acc[:, HEAD : HEAD + 1]
        return _

    lax.fori_loop(0, 2, attend, 0)
    got[me] = pa_ref[me]
    settle(me, pa_ref, got, (front_send1, front_recv1))

    keeps = [kept(lens_ref, i) for i in range(SEQ)]
    state = jnp.zeros((HEAD // 2, HEAD), f32)
    for i in range(SEQ):
        outs[i] = state.astype(bf16)
        block = got[i]
        hops_ref[i] = block[:HEAD]
        hop = block[:HEAD]
        state = keeps[i] * state + d2(state, hop, NN) + block[HEAD:].astype(f32)
    for turn in range(2):
        spread(me, outs, s_in, (front_send2, front_recv2), team_peers(me, turn))
    s_in[me] = outs[me]
    lax.fori_loop(2, 4, attend, 0)
    settle(me, outs, s_in, (front_send2, front_recv2))
    for h in range(HEADS):
        state = jnp.concatenate([s_in[2 * h], s_in[2 * h + 1]], axis=0)
        s_ref[h] = state
        gap = lead * d3(qe_ref[h], state, NT) + grad_ref[:, h * HEAD : (h + 1) * HEAD]
        gap_ref[:, h * HEAD : (h + 1) * HEAD] = gap.astype(bf16)
    for copy in across + whole_rows + far_rows:
        copy.wait_send()

    def send(source, target, peer, send_sem, recv_sem):
        copy = remote(source, target, send_sem, recv_sem, peer, "head")
        copy.start()
        return copy

    gap = gap_ref[...]

    def part(side, quarter, half):
        weight_copy(side, quarter, half).wait()
        return mm(gap, w[side * 8 + quarter * 2 + half], NN)

    sib = []

    def send_pair(n):
        for half in range(2):
            sib_out[n, half] = part(1 - core, order[n], half).astype(bf16)
        sib.append(send(sib_out.at[n], sib_in.at[n], sibling, sib_send.at[n], sib_recv.at[n]))

    def pair(n, half):
        return part(core, order[n], half) + sib_in[n, half].astype(f32)

    def scatter(source, target, peer, n):
        return send(source, target, peer, rs_send.at[n], rs_recv.at[n])

    send_pair(0)
    send_pair(1)
    sib[0].wait_recv()
    far[0] = pair(0, 0).astype(bf16)
    send_a = scatter(far.at[0], in_a, above, 0)
    far[1] = pair(0, 1).astype(bf16)
    send_b = scatter(far.at[1], in_b, below, 1)
    send_pair(2)
    send_pair(3)
    sib[1].wait_recv()
    up[1] = pair(1, 1).astype(bf16)
    up_1 = scatter(up.at[1], in_up.at[1], above, 2)
    sib[2].wait_recv()
    down[0] = pair(2, 0).astype(bf16)
    down_0 = scatter(down.at[0], in_down.at[0], below, 3)
    first_up = pair(1, 0)
    send_a.wait_recv()
    up[0] = (first_up + in_a[...].astype(f32)).astype(bf16)
    up_0 = scatter(up.at[0], in_up.at[0], above, 4)
    first_down = pair(2, 1)
    send_b.wait_recv()
    down[1] = (first_down + in_b[...].astype(f32)).astype(bf16)
    down_1 = scatter(down.at[1], in_down.at[1], below, 5)
    sib[3].wait_recv()
    mine = [pair(3, 0), pair(3, 1)]
    own = core * 4 + z

    def gather(chunk, half, peer, n):
        ref = r.at[chunk] if half is None else r.at[chunk, half]
        return send(ref, ref, peer, ag_send.at[n], ag_recv.at[n])

    def settle_own(half, early, late):
        early.wait_recv()
        late.wait_recv()
        total = mine[half] + (in_up[half].astype(f32) + in_down[half].astype(f32))
        r[own, half] = total.astype(bf16)

    settle_own(0, down_0, up_0)
    own_up_0 = gather(own, 0, above, 0)
    settle_own(1, up_1, down_1)
    own_down_1 = gather(own, 1, below, 1)
    own_up_1 = gather(own, 1, above, 2)
    own_down_0 = gather(own, 0, below, 3)
    own_sib = gather(own, None, sibling, 4)

    loss_ref[...] = jnp.zeros_like(loss_ref)

    def use(chunk, half, first=False):
        block = r[chunk, half]
        term = 2.0 * mm(block, w[chunk * 2 + half], NT)
        grad_ref[...] = term if first else grad_ref[...] + term
        wide = block.astype(f32)
        loss_ref[...] += jnp.sum(wide * wide, axis=0, keepdims=True)

    sides = core * 4
    others = (1 - core) * 4
    use(own, 0, True)
    use(own, 1)
    own_sib.wait_recv()
    use(others + z, 0)
    own_up_0.wait_recv()
    pass_a = gather(sides + zm, 0, above, 5)
    own_down_1.wait_recv()
    pass_b = gather(sides + zp, 1, below, 6)
    use(others + z, 1)
    own_up_1.wait_recv()
    sib_m = gather(sides + zm, None, sibling, 7)
    own_down_0.wait_recv()
    sib_p = gather(sides + zp, None, sibling, 8)
    use(sides + zm, 0)
    use(sides + zm, 1)
    use(sides + zp, 0)
    use(sides + zp, 1)
    sib_m.wait_recv()
    use(others + zm, 0)
    use(others + zm, 1)
    sib_p.wait_recv()
    use(others + zp, 0)
    use(others + zp, 1)
    pass_a.wait_recv()
    sib_a = gather(sides + z2, 0, sibling, 9)
    pass_b.wait_recv()
    sib_b = gather(sides + z2, 1, sibling, 10)
    use(sides + z2, 0)
    use(sides + z2, 1)
    sib_a.wait_recv()
    use(others + z2, 0)
    sib_b.wait_recv()
    use(others + z2, 1)
    for copy in sib + [
        send_a, send_b, up_0, up_1, down_0, down_1, own_up_0, own_up_1, own_down_0, own_down_1,
        own_sib, pass_a, sib_m, pass_b, sib_p, sib_a, sib_b,
    ]:
        copy.wait_send()
    half = HEAD // 2

    def state_grads(turn, _):
        for n in team:
            h = turn * TEAM + n
            ds = d3(lead * grad_ref[:, lanes(h)], qe_ref[h], TN).astype(bf16)
            ds_ref[2 * h] = ds[:half]
            ds_ref[2 * h + 1] = ds[half:]
        spread(me, ds_ref, ds_got, (send1, recv1), team_peers(me, turn))
        return _

    lax.fori_loop(0, HEADS // TEAM, state_grads, 0)

    def query_side(turn, _):
        heads = [turn * TEAM + n for n in team]
        gs = [grad_ref[:, lanes(h)] for h in heads]
        dqes = [d3(lead * g, s_ref[h], NN) for h, g in zip(heads, gs)]
        boths = [jnp.concatenate([-dqe, g], axis=1) for dqe, g in zip(dqes, gs)]
        dscs = [jnp.where(allowed, d3(b, w_ref[h], NT), 0.0) for h, b in zip(heads, boths)]
        for h, both in zip(heads, boths):
            sc_ref[h] = d3(sc_ref[h], both, TN)
        for n, h in enumerate(heads):
            zq = zq_ref[h]
            qe_ref[h] = d3(dscs[n], unit(zq), TN)
            dqu = dqes[n] + d3(dscs[n], unit(zk_ref[h]), NN)
            dqm = d2r(q_ref[:, lanes(h)], unit_back(zq, dqu), TN)
            pq[2 * h] = dqm[:half]
            pq[2 * h + 1] = dqm[half:]
        return _

    query_side(0, 0)
    ds_got[me] = ds_ref[me]
    settle(me, ds_ref, ds_got, (send1, recv1))

    keeps = [kept(lens_ref, i) for i in range(SEQ)]
    state = jnp.zeros((half, HEAD), f32)
    for i in reversed(range(SEQ)):
        outs[i] = state.astype(bf16)
        state = keeps[i] * state + d2(state, hops_ref[i], NT) + ds_got[i].astype(f32)
    for turn in range(2):
        spread(me, outs, lam_ref, (send2, recv2), team_peers(me, turn))
    lam_ref[me] = outs[me]
    query_side(1, 0)
    spread(me, pq, pq_got, (send3, recv3), [p for _, p in seq_peers(me)])

    settle(me, outs, lam_ref, (send2, recv2))

    loss = jnp.broadcast_to(jnp.sum(loss_ref[...], axis=1, keepdims=True), (1, HEAD))

    key_sems = [(send5, recv5), (send7, recv7)]
    share_sems = [(send6, recv6), (send8, recv8)]

    def key_total(turn):
        pk_got[turn, me] = pk[turn, me]
        settle(me, pk.at[turn], pk_got.at[turn], key_sems[turn])
        total = pk_got[turn, 0]
        for i in range(1, SEQ):
            total = total + pk_got[turn, i]
        pk_own[turn] = total[:32].astype(bf16)
        row_ref[turn * TEAM : (turn + 1) * TEAM] = total[32:36]
        share(me, pk_own.at[turn], pk_all.at[turn], share_sems[turn])
        pk_all[turn, me] = pk_own[turn]
        return total

    def key_side(turn):
        heads = [turn * TEAM + n for n in team]
        lams = [jnp.concatenate([lam_ref[2 * h], lam_ref[2 * h + 1]], axis=0) for h in heads]
        kus = [unit(zk_ref[h]) for h in heads]
        ws = [w_ref[h] for h in heads]
        dhops = [lead_last * mm(s_ref[h], lams[n], TN) for n, h in enumerate(heads)]
        drs = []
        for n, h in enumerate(heads):
            dwk = sc_ref[h, :, :HEAD] - d3(kus[n], dhops[n], NT)
            dwv = sc_ref[h, :, HEAD:] + tail * d2(kus[n], lams[n], NT)
            drs.append(d3(t_ref[h], jnp.concatenate([dwk, dwv], axis=1), TN))
        dkus = [
            qe_ref[h]
            - d3(ws[n][:, :HEAD], dhops[n], NN)
            + tail * d2(ws[n][:, HEAD:], lams[n], NN)
            for n, h in enumerate(heads)
        ]
        dlows = [jnp.where(strict, -d3(drs[n], ws[n], NT), 0.0) for n in team]
        kterms = [drs[n][:, :HEAD] + d3(dlows[n], kus[n], NN) for n in team]
        dkm_rows, extra = [], []
        for n, h in enumerate(heads):
            beta = beta_ref[h]
            dbeta = jnp.sum(kterms[n] * kus[n] + drs[n][:, HEAD:] * v, axis=-1, keepdims=True)
            dku = dkus[n] + beta * kterms[n] + d3(beta * dlows[n], kus[n], TN)
            dkm = d2r(k, unit_back(zk_ref[h], dku), TN)
            dlogit = dbeta * beta * (1.0 - beta)
            q = q_ref[:, lanes(h)].astype(f32)
            dkm_rows.append(dkm.reshape(SEQ, 8, HEAD))
            extra.append(jnp.sum(q * dlogit, axis=0, keepdims=True))
        extra = jnp.concatenate(extra + [loss, jnp.zeros((3, HEAD), f32)], axis=0)
        pk[turn, :, :32] = jnp.concatenate(dkm_rows, axis=1)
        pk[turn, :, 32:] = jnp.broadcast_to(extra[None], (SEQ, 8, HEAD))
        spread(me, pk.at[turn], pk_got.at[turn], key_sems[turn], [p for _, p in seq_peers(me)])

    key_side(0)
    pq_got[me] = pq[me]
    settle(me, pq, pq_got, (send3, recv3))
    pq_own[...] = lax.fori_loop(
        0, SEQ, lambda i, total: total + pq_got[i], jnp.zeros((half, HEAD), f32)
    ).astype(bf16)
    share(me, pq_own, pq_all, (send4, recv4))
    pq_all[me] = pq_own[...]
    key_side(1)
    key_total(0)
    total = key_total(1)
    loss_out[...] = total[36:37]
    settle_share(me, pq_own, pq_all, (send4, recv4))
    dq_ref[...] = pq_all[...]
    for turn in range(2):
        settle_share(me, pk_own.at[turn], pk_all.at[turn], share_sems[turn])
    dk_ref[...] = pk_all[...]


def finish_kernel(dq_in, dk_in, row_in, loss_in, dq_ref, dk_ref, row_ref, loss_ref):
    dq_ref[...] = dq_in[...].astype(f32)
    for turn in range(HEADS // TEAM):
        wide = dk_in[turn].astype(f32)
        for n in range(TEAM):
            dk_ref[turn * TEAM + n] = wide[:, n * 8 : (n + 1) * 8].reshape(HEAD, HEAD)
    row_ref[...] = row_in[...]
    loss_ref[...] = loss_in[:, :1] / (SEQ * ROWS * WIDTH)


def shape(dims, dtype):
    return jax.ShapeDtypeStruct(dims, dtype)


SMEM = pl.BlockSpec(memory_space=pltpu.SMEM)
VMEM = pl.BlockSpec(memory_space=pltpu.VMEM)
ANY = pl.BlockSpec(memory_space=pl.ANY)


def params(**more):
    return pltpu.CompilerParams(vmem_limit_bytes=VMEM_BYTES, has_side_effects=True, **more)


def shards(q, k, v, lens, proj, query_map, key_map, beta_weight, beta_bias):
    bw = beta_weight.reshape(HEADS, 1, HEAD)
    square = (HEADS, ROWS, ROWS)
    slab = (HEADS, ROWS, HEAD)
    halves = (SEQ, HEAD // 2, HEAD)
    extended = (2, SEQ, 40, HEAD)
    shares = (2, SEQ, 32, HEAD)
    block = (2, ROWS, HALF)
    scratch = [
        (slab, f32), (slab, f32), ((HEADS, ROWS, 1), f32), (square, f32), (square, f32),
        (square, f32), (slab, f32), ((ROWS, HEADS * HEAD), f32),
        ((1, HALF), f32), ((ROWS, HEADS * HEAD), bf16), ((HEADS, HEAD, HEAD), bf16),
        ((SEQ, HEAD, HEAD), bf16),
        ((SEQ, 192, HEAD), bf16), ((SEQ, 192, HEAD), bf16), (halves, bf16),
        ((4, 4, ROWS, HEAD), bf16), ((4, 4, ROWS, HEAD), bf16),
        (halves, bf16), (halves, bf16), (halves, bf16), (halves, bf16),
        (halves, f32), (halves, f32), (halves[1:], bf16), (halves, bf16),
        (extended, f32), (extended, f32), ((2, 32, HEAD), bf16), (shares, bf16),
        ((16, HEADS * HEAD, HALF), bf16), ((4,) + block, bf16), ((4,) + block, bf16),
        (block, bf16), (block, bf16), (block, bf16), (block[1:], bf16), (block[1:], bf16),
        (block, bf16), (block, bf16), ((8,) + block, bf16),
    ]
    sems = [16, 4, 4, 6, 6, 11, 11] + [SEQ] * 22
    partial = pl.pallas_call(
        whole_kernel,
        in_specs=[SMEM, SMEM] + [VMEM] * 6 + [ANY],
        out_specs=[VMEM] * 4,
        out_shape=[
            shape(halves, bf16), shape(shares, bf16), shape((HEADS, HEAD), f32),
            shape((1, HEAD), f32),
        ],
        scratch_shapes=[pltpu.VMEM(dims, kind) for dims, kind in scratch]
        + [pltpu.SemaphoreType.DMA((count,)) for count in sems],
        compiler_params=params(collective_id=0),
        name="whole",
    )(lens, beta_bias, q, k, v, query_map, key_map, bw, proj)
    grad_query, grad_key, grad_beta, loss = pl.pallas_call(
        finish_kernel,
        in_specs=[VMEM] * 4,
        out_specs=[VMEM] * 4,
        out_shape=[
            shape(halves, f32), shape((HEADS, HEAD, HEAD), f32), shape((HEADS, HEAD), f32),
            shape((1, 1), f32),
        ],
        name="finish",
    )(*partial)
    return loss.reshape(()), grad_query.reshape(HEADS, HEAD, HEAD), grad_key, grad_beta


def solution(mesh):
    return jax.shard_map(
        shards,
        mesh=mesh,
        in_specs=(
            P("seq", "head"),
            P("seq", "head"),
            P("seq", "head"),
            P(),
            P("head", None),
            P("head", None, None),
            P("head", None, None),
            P("head", None),
            P("head"),
        ),
        out_specs=(P(), P("head", None, None), P("head", None, None), P("head", None)),
        check_vma=False,
    )
```

```python
import functools
import math

import jax
import jax.numpy as jnp
from jax import lax
from jax.experimental import pallas as pl
from jax.experimental.pallas import tpu as pltpu
from jax.sharding import PartitionSpec as P

HEAD = 128
ROWS = 256
HEADS = 8
SEQ = 16
NDOCS = 8
WIDTH = 8192
HALF = 512
KEY_BLOCK = 2048
TEAM = 4

f32 = jnp.float32
bf16 = jnp.bfloat16
NN = ((1,), (0,))
NT = ((1,), (1,))
TN = ((0,), (0,))
VMEM_BYTES = 62 * 1024 * 1024
MESH = pl.DeviceIdType.MESH


def mm(a, b, dims):
    return lax.dot_general(a, b, (dims, ((), ())), preferred_element_type=f32)


def split(x):
    hi = x.astype(bf16)
    return hi, (x - hi.astype(f32)).astype(bf16)


def d1(a, b, dims):
    return mm(a.astype(bf16), b.astype(bf16), dims)


def d3(a, b, dims):
    ah, al = split(a)
    bh, bl = split(b)
    return mm(ah, bh, dims) + (mm(ah, bl, dims) + mm(al, bh, dims))


def d2(a, b, dims):
    ah, al = split(a)
    return mm(ah, b, dims) + mm(al, b, dims)


def d2r(a, b, dims):
    bh, bl = split(b)
    return mm(a, bh, dims) + mm(a, bl, dims)


def row_starts(lens_ref, first_row):
    t = lax.broadcasted_iota(jnp.int32, (ROWS, 1), 0) + first_row
    start = jnp.zeros((ROWS, 1), jnp.int32)
    at = jnp.int32(0)
    for doc in range(NDOCS):
        start = jnp.where(t >= at, at, start)
        at = at + lens_ref[doc]
    return start - first_row


def iotas():
    return (
        lax.broadcasted_iota(jnp.int32, (ROWS, ROWS), 0),
        lax.broadcasted_iota(jnp.int32, (ROWS, ROWS), 1),
    )


def sigmoid(z):
    return 1.0 / (1.0 + jnp.exp(-z))


def unit(z):
    act = z * sigmoid(z)
    scale = lax.rsqrt(jnp.sum(act * act, axis=-1, keepdims=True) + 1e-06)
    return act * scale


def unit_back(z, grad):
    gate = sigmoid(z)
    act = z * gate
    scale = lax.rsqrt(jnp.sum(act * act, axis=-1, keepdims=True) + 1e-06)
    out = act * scale
    act_grad = scale * (grad - out * jnp.sum(out * grad, axis=-1, keepdims=True))
    return act_grad * (gate * (1.0 + z * (1.0 - gate)))


def lower_inverses(lows, ri, ci):
    half = ROWS // 2
    eye = (ri == ci).astype(f32)
    r, c = ri[:half, :half], ci[:half, :half]
    parts = [p for low in lows for p in (low[:half, :half], low[half:, half:])]
    small = eye[:half, :half]
    near = (r >> 1) == (c >> 1)
    invs = [small - jnp.where(near, p, 0.0) for p in parts]
    parts = [p.astype(bf16) for p in parts]
    for k in range(1, 7):
        ring = ((r >> (k + 1)) == (c >> (k + 1))) & ((r >> k) != (c >> k))
        inv16 = [inv.astype(bf16) for inv in invs]
        mids = [
            mm(jnp.where(ring, p, jnp.zeros_like(p)), i, NN).astype(bf16)
            for p, i in zip(parts, inv16)
        ]
        invs = [inv - mm(i, mid, NN) for inv, i, mid in zip(invs, inv16, mids)]
    whole = []
    for n, low in enumerate(lows):
        top, bottom = invs[2 * n], invs[2 * n + 1]
        corner = -d1(d1(bottom, low[half:, :half], NN), top, NN)
        upper = jnp.concatenate([top, jnp.zeros((half, half), f32)], axis=1)
        lower = jnp.concatenate([corner, bottom], axis=1)
        whole.append(jnp.concatenate([upper, lower], axis=0))
    misses = [(eye - inv) - d3(low, inv, NN) for low, inv in zip(lows, whole)]
    return [inv + d1(inv, miss, NN) for inv, miss in zip(whole, misses)]


def kept(lens_ref, i):
    start = jnp.int32(0)
    at = jnp.int32(0)
    for doc in range(NDOCS):
        start = jnp.where((i + 1) * ROWS > at, at, start)
        at = at + lens_ref[doc]
    return jnp.where(start < i * ROWS, 1.0, 0.0).astype(f32)


def signal_all(peers):
    barrier = pltpu.get_barrier_semaphore()
    for axis, index in peers:
        pl.semaphore_signal(barrier, inc=1, device_id={axis: index}, device_id_type=MESH)
    pl.semaphore_wait(barrier, len(peers))


def seq_peers(me):
    return [("seq", lax.rem(me + hop, SEQ)) for hop in range(1, SEQ)]


def remote(source, target, send_sem, recv_sem, peer, axis="seq"):
    return pltpu.make_async_remote_copy(
        src_ref=source,
        dst_ref=target,
        send_sem=send_sem,
        recv_sem=recv_sem,
        device_id={axis: peer},
        device_id_type=MESH,
    )


def spread(me, source, target, sems, peers):
    send, recv = sems
    for peer in peers:

        @pl.when(peer != me)
        def _(peer=peer):
            remote(source.at[peer], target.at[me], send.at[peer], recv.at[me], peer).start()


def team_peers(me, team):
    return [team * 8 + lax.rem(me + n, 8) for n in range(8)]


def settle(me, source, target, sems):
    send, recv = sems
    for hop in range(1, SEQ):
        peer = lax.rem(me + hop, SEQ)
        remote(source.at[peer], target.at[peer], send.at[peer], recv.at[peer], peer).wait()


def share(me, source, target, sems):
    send, recv = sems
    for hop in range(1, SEQ):
        peer = lax.rem(me + hop, SEQ)
        remote(source, target.at[me], send.at[peer], recv.at[me], peer).start()


def settle_share(me, source, target, sems):
    send, recv = sems
    for hop in range(1, SEQ):
        peer = lax.rem(me + hop, SEQ)
        remote(source, target.at[peer], send.at[peer], recv.at[peer], peer).wait()


def lanes(head):
    return pl.ds(pl.multiple_of(head * HEAD, HEAD), HEAD)


PAIR = 2


def whole_kernel(
    lens_ref, bias_ref, q_ref, k_ref, v_ref, qm_ref, km_ref, bw_ref, proj_ref,
    dq_ref, dk_ref, row_ref, loss_out,
    zq_ref, zk_ref, beta_ref, t_ref, w_ref, sc_ref, qe_ref, grad_ref,
    loss_ref, gap_ref, s_ref, hops_ref,
    pa_ref, got, s_in, keys_at, values_at,
    ds_ref, ds_got, outs, lam_ref, pq, pq_got, pq_own, pq_all, pk, pk_got, pk_own, pk_all,
    w, sib_out, sib_in, far, up, down, in_a, in_b, in_up, in_down, r,
    w_sem, sib_send, sib_recv, rs_send, rs_recv, ag_send, ag_recv,
    kv_send, kv_recv, front_send1, front_recv1, front_send2, front_recv2,
    send1, recv1, send2, recv2, send3, recv3, send4, recv4, send5, recv5, send6, recv6,
    send7, recv7, send8, recv8,
):
    me = lax.axis_index("seq")
    head = lax.axis_index("head")
    z, core = head // 2, lax.rem(head, 2)
    zp, zm, z2 = lax.rem(z + 1, 4), lax.rem(z + 3, 4), lax.rem(z + 2, 4)
    above, below, sibling = zp * 2 + core, zm * 2 + core, z * 2 + (1 - core)
    order = (z2, zp, zm, z)

    def weight_copy(side, quarter, half):
        at = side * 8 + quarter * 2 + half
        return pltpu.make_async_copy(
            proj_ref.at[:, pl.ds(pl.multiple_of(at * HALF, HALF), HALF)], w.at[at], w_sem.at[at]
        )

    first = me * ROWS
    k = k_ref[...]
    v16 = v_ref[...]
    v = v16.astype(f32)
    x, y = me // 4, lax.rem(me, 4)
    xp, xm, yp, ym = lax.rem(x + 1, 4), lax.rem(x + 3, 4), lax.rem(y + 1, 4), lax.rem(y + 3, 4)
    keys_at[x, y] = k
    values_at[y, x] = v16
    for side in (1 - core, core):
        for quarter in order:
            for half in range(2):
                weight_copy(side, quarter, half).start()
    signal_all([("head", above), ("head", below), ("head", sibling)] + seq_peers(me))

    def relay(n, source, peer):
        return remote(source, source, kv_send.at[n], kv_recv.at[n], peer)

    across = []
    for d in range(1, 4):
        across.append(relay(d - 1, keys_at.at[x, y], x * 4 + lax.rem(y + d, 4)))
        across.append(relay(d + 2, values_at.at[y, x], lax.rem(x + d, 4) * 4 + y))
    whole_rows = [
        relay(6, keys_at.at[x], xp * 4 + y),
        relay(7, keys_at.at[x], xm * 4 + y),
        relay(8, values_at.at[y], x * 4 + yp),
        relay(9, values_at.at[y], x * 4 + ym),
    ]
    far_rows = [
        relay(10, keys_at.at[xm, pl.ds(0, 2)], xp * 4 + y),
        relay(11, keys_at.at[xp, pl.ds(2, 2)], xm * 4 + y),
        relay(12, values_at.at[ym, pl.ds(0, 2)], x * 4 + yp),
        relay(13, values_at.at[yp, pl.ds(2, 2)], x * 4 + ym),
    ]
    for copy in across:
        copy.start()

    def pass_on(turn):
        @pl.when(turn == 0)
        def _():
            for copy in across:
                copy.wait_recv()
            for copy in whole_rows:
                copy.start()

        @pl.when(turn == 1)
        def _():
            for copy in whole_rows:
                copy.wait_recv()
            for copy in far_rows:
                copy.start()

    start = row_starts(lens_ref, first)
    lead = (start < 0).astype(f32)
    lead_last = lead[ROWS - 1 :, :]
    tail = (start == start[ROWS - 1 :, :]).astype(f32)
    ri, ci = iotas()
    allowed = (ci <= ri) & (ci >= start)
    strict = (ci < ri) & (ci >= start)
    team = range(TEAM)

    def prepare(turn, _):
        heads = [turn * TEAM + n for n in team]
        qus, kus, betas = [], [], []
        for h in heads:
            q = q_ref[:, lanes(h)]
            qh, ql = split(qm_ref[h])
            kh, kl = split(km_ref[h])
            zq = mm(q, qh, NN) + mm(q, ql, NN)
            zk = mm(k, kh, NN) + mm(k, kl, NN)
            zq_ref[h] = zq
            zk_ref[h] = zk
            logits = jnp.sum(q.astype(f32) * bw_ref[h], axis=-1, keepdims=True)
            beta = sigmoid(logits + bias_ref[h])
            beta_ref[h] = beta
            qus.append(unit(zq))
            kus.append(unit(zk))
            betas.append(beta)
        lows = [jnp.where(strict, betas[n] * d3(kus[n], kus[n], NT), 0.0) for n in team]
        invs = lower_inverses(lows, ri, ci)
        pass_on(turn)
        ws = [
            d3(invs[n], jnp.concatenate([betas[n] * kus[n], betas[n] * v], axis=1), NN)
            for n in team
        ]
        scores = [jnp.where(allowed, d3(qus[n], kus[n], NT), 0.0) for n in team]
        for n, h in enumerate(heads):
            t_ref[h] = invs[n]
            w_ref[h] = ws[n]
            sc_ref[h] = scores[n]
            mixed = d3(scores[n], ws[n], NN)
            qe_ref[h] = qus[n] - mixed[:, :HEAD]
            grad_ref[:, lanes(h)] = mixed[:, HEAD:]
            both = jnp.concatenate([ws[n][:, :HEAD], tail * ws[n][:, HEAD:]], axis=1)
            pair = d3(both, kus[n], TN)
            hop = (-lead_last * pair[:HEAD]).astype(bf16)
            add = pair[HEAD:].astype(bf16)
            for side in range(2):
                pa_ref[2 * h + side, :HEAD] = hop
                pa_ref[2 * h + side, HEAD:] = add[side * (HEAD // 2) : (side + 1) * (HEAD // 2)]
        spread(me, pa_ref, got, (front_send1, front_recv1), team_peers(me, turn))
        return _

    lax.fori_loop(0, HEADS // TEAM, prepare, 0)
    for copy in far_rows:
        copy.wait_recv()
    scale = math.log2(math.e) / math.sqrt(HEAD)
    row = lax.broadcasted_iota(jnp.int32, (ROWS, 1), 0)
    lane = lax.broadcasted_iota(jnp.int32, (1, KEY_BLOCK), 1)

    def attend(turn, _):
        queries = []
        for n in range(PAIR):
            hi, lo = split(q_ref[:, lanes(turn * PAIR + n)].astype(f32) * scale)
            queries.append(jnp.concatenate([hi, lo], axis=1))
        query = jnp.concatenate(queries, axis=0)

        def step(block, carry):
            keys = keys_at[pl.ds(2 * block, 2)].reshape(KEY_BLOCK, HEAD)
            keys = jnp.concatenate([keys, keys], axis=1)
            values = jnp.concatenate(
                [values_at[n, 2 * block + at] for at in range(2) for n in range(4)], axis=0
            )
            values = jnp.concatenate([values, jnp.ones((KEY_BLOCK, HEAD), bf16)], axis=1)
            u = lane + (block * KEY_BLOCK - first)
            seen = (u >= start) & (u <= row)
            scores = mm(query, keys, NT)
            out = []
            for n, (peak, acc) in enumerate(carry):
                s = jnp.where(seen, scores[n * ROWS : (n + 1) * ROWS], -1e30)
                new = jnp.maximum(peak, jnp.max(s, axis=-1, keepdims=True))
                weights = jnp.exp2(s - new).astype(bf16)
                out.append((new, acc * jnp.exp2(peak - new) + mm(weights, values, NN)))
            return tuple(out)

        carry = tuple(
            (jnp.full((ROWS, 1), -1e30, f32), jnp.zeros((ROWS, 2 * HEAD), f32))
            for _ in range(PAIR)
        )
        carry = lax.fori_loop(0, (first + ROWS - 1) // KEY_BLOCK + 1, step, carry)
        for n in range(PAIR):
            acc = carry[n][1]
            grad_ref[:, lanes(turn * PAIR + n)] -= acc[:, :HEAD] / acc[:, HEAD : HEAD + 1]
        return _

    lax.fori_loop(0, 2, attend, 0)
    got[me] = pa_ref[me]
    settle(me, pa_ref, got, (front_send1, front_recv1))

    keeps = [kept(lens_ref, i) for i in range(SEQ)]
    state = jnp.zeros((HEAD // 2, HEAD), f32)
    for i in range(SEQ):
        outs[i] = state.astype(bf16)
        block = got[i]
        hops_ref[i] = block[:HEAD]
        hop = block[:HEAD]
        state = keeps[i] * state + d2(state, hop, NN) + block[HEAD:].astype(f32)
    for turn in range(2):
        spread(me, outs, s_in, (front_send2, front_recv2), team_peers(me, turn))
    s_in[me] = outs[me]
    lax.fori_loop(2, 4, attend, 0)
    settle(me, outs, s_in, (front_send2, front_recv2))
    for h in range(HEADS):
        state = jnp.concatenate([s_in[2 * h], s_in[2 * h + 1]], axis=0)
        s_ref[h] = state
        gap = lead * d3(qe_ref[h], state, NT) + grad_ref[:, h * HEAD : (h + 1) * HEAD]
        gap_ref[:, h * HEAD : (h + 1) * HEAD] = gap.astype(bf16)
    for copy in across + whole_rows + far_rows:
        copy.wait_send()

    def send(source, target, peer, send_sem, recv_sem):
        copy = remote(source, target, send_sem, recv_sem, peer, "head")
        copy.start()
        return copy

    gap = gap_ref[...]

    def part(side, quarter, half):
        weight_copy(side, quarter, half).wait()
        return mm(gap, w[side * 8 + quarter * 2 + half], NN)

    sib = []

    def send_pair(n):
        for half in range(2):
            sib_out[n, half] = part(1 - core, order[n], half).astype(bf16)
        sib.append(send(sib_out.at[n], sib_in.at[n], sibling, sib_send.at[n], sib_recv.at[n]))

    def pair(n, half):
        return part(core, order[n], half) + sib_in[n, half].astype(f32)

    def scatter(source, target, peer, n):
        return send(source, target, peer, rs_send.at[n], rs_recv.at[n])

    send_pair(0)
    send_pair(1)
    sib[0].wait_recv()
    far[0] = pair(0, 0).astype(bf16)
    send_a = scatter(far.at[0], in_a, above, 0)
    far[1] = pair(0, 1).astype(bf16)
    send_b = scatter(far.at[1], in_b, below, 1)
    send_pair(2)
    send_pair(3)
    sib[1].wait_recv()
    up[1] = pair(1, 1).astype(bf16)
    up_1 = scatter(up.at[1], in_up.at[1], above, 2)
    sib[2].wait_recv()
    down[0] = pair(2, 0).astype(bf16)
    down_0 = scatter(down.at[0], in_down.at[0], below, 3)
    first_up = pair(1, 0)
    send_a.wait_recv()
    up[0] = (first_up + in_a[...].astype(f32)).astype(bf16)
    up_0 = scatter(up.at[0], in_up.at[0], above, 4)
    first_down = pair(2, 1)
    send_b.wait_recv()
    down[1] = (first_down + in_b[...].astype(f32)).astype(bf16)
    down_1 = scatter(down.at[1], in_down.at[1], below, 5)
    sib[3].wait_recv()
    mine = [pair(3, 0), pair(3, 1)]
    own = core * 4 + z

    def gather(chunk, half, peer, n):
        ref = r.at[chunk] if half is None else r.at[chunk, half]
        return send(ref, ref, peer, ag_send.at[n], ag_recv.at[n])

    def settle_own(half, early, late):
        early.wait_recv()
        late.wait_recv()
        total = mine[half] + (in_up[half].astype(f32) + in_down[half].astype(f32))
        r[own, half] = total.astype(bf16)

    settle_own(0, down_0, up_0)
    own_up_0 = gather(own, 0, above, 0)
    settle_own(1, up_1, down_1)
    own_down_1 = gather(own, 1, below, 1)
    own_up_1 = gather(own, 1, above, 2)
    own_down_0 = gather(own, 0, below, 3)
    own_sib = gather(own, None, sibling, 4)

    loss_ref[...] = jnp.zeros_like(loss_ref)

    def use(chunk, *halves, first=False):
        term, squares = None, 0.0
        for half in halves:
            block = r[chunk, half]
            wide = block.astype(f32)
            squares += jnp.sum(wide * wide, axis=0, keepdims=True)
            product = mm(block + block, w[chunk * 2 + half], NT)
            term = product if term is None else term + product
        grad_ref[...] = term if first else grad_ref[...] + term
        loss_ref[...] += squares

    sides = core * 4
    others = (1 - core) * 4
    use(own, 0, 1, first=True)
    own_sib.wait_recv()
    use(others + z, 0)
    own_up_0.wait_recv()
    pass_a = gather(sides + zm, 0, above, 5)
    own_down_1.wait_recv()
    pass_b = gather(sides + zp, 1, below, 6)
    use(others + z, 1)
    own_up_1.wait_recv()
    sib_m = gather(sides + zm, None, sibling, 7)
    own_down_0.wait_recv()
    sib_p = gather(sides + zp, None, sibling, 8)
    use(sides + zm, 0, 1)
    use(sides + zp, 0, 1)
    sib_m.wait_recv()
    use(others + zm, 0, 1)
    sib_p.wait_recv()
    use(others + zp, 0, 1)
    pass_a.wait_recv()
    sib_a = gather(sides + z2, 0, sibling, 9)
    pass_b.wait_recv()
    sib_b = gather(sides + z2, 1, sibling, 10)
    use(sides + z2, 0, 1)
    sib_a.wait_recv()
    use(others + z2, 0)
    sib_b.wait_recv()
    use(others + z2, 1)
    for copy in sib + [
        send_a, send_b, up_0, up_1, down_0, down_1, own_up_0, own_up_1, own_down_0, own_down_1,
        own_sib, pass_a, sib_m, pass_b, sib_p, sib_a, sib_b,
    ]:
        copy.wait_send()
    half = HEAD // 2

    def state_grads(turn, _):
        for n in team:
            h = turn * TEAM + n
            ds = d3(lead * grad_ref[:, lanes(h)], qe_ref[h], TN).astype(bf16)
            ds_ref[2 * h] = ds[:half]
            ds_ref[2 * h + 1] = ds[half:]
        spread(me, ds_ref, ds_got, (send1, recv1), team_peers(me, turn))
        return _

    lax.fori_loop(0, HEADS // TEAM, state_grads, 0)

    def query_side(turn, _):
        heads = [turn * TEAM + n for n in team]
        gs = [grad_ref[:, lanes(h)] for h in heads]
        dqes = [d3(lead * g, s_ref[h], NN) for h, g in zip(heads, gs)]
        boths = [jnp.concatenate([-dqe, g], axis=1) for dqe, g in zip(dqes, gs)]
        dscs = [jnp.where(allowed, d3(b, w_ref[h], NT), 0.0) for h, b in zip(heads, boths)]
        for h, both in zip(heads, boths):
            sc_ref[h] = d3(sc_ref[h], both, TN)
        for n, h in enumerate(heads):
            zq = zq_ref[h]
            qe_ref[h] = d3(dscs[n], unit(zq), TN)
            dqu = dqes[n] + d3(dscs[n], unit(zk_ref[h]), NN)
            dqm = d2r(q_ref[:, lanes(h)], unit_back(zq, dqu), TN)
            pq[2 * h] = dqm[:half]
            pq[2 * h + 1] = dqm[half:]
        return _

    query_side(0, 0)
    ds_got[me] = ds_ref[me]
    settle(me, ds_ref, ds_got, (send1, recv1))

    keeps = [kept(lens_ref, i) for i in range(SEQ)]
    state = jnp.zeros((half, HEAD), f32)
    for i in reversed(range(SEQ)):
        outs[i] = state.astype(bf16)
        state = keeps[i] * state + d2(state, hops_ref[i], NT) + ds_got[i].astype(f32)
    for turn in range(2):
        spread(me, outs, lam_ref, (send2, recv2), team_peers(me, turn))
    lam_ref[me] = outs[me]
    query_side(1, 0)
    spread(me, pq, pq_got, (send3, recv3), [p for _, p in seq_peers(me)])

    settle(me, outs, lam_ref, (send2, recv2))

    loss = jnp.broadcast_to(jnp.sum(loss_ref[...], axis=1, keepdims=True), (1, HEAD))

    key_sems = [(send5, recv5), (send7, recv7)]
    share_sems = [(send6, recv6), (send8, recv8)]

    def key_total(turn):
        pk_got[turn, me] = pk[turn, me]
        settle(me, pk.at[turn], pk_got.at[turn], key_sems[turn])
        total = pk_got[turn, 0]
        for i in range(1, SEQ):
            total = total + pk_got[turn, i]
        pk_own[turn] = total[:32].astype(bf16)
        row_ref[turn * TEAM : (turn + 1) * TEAM] = total[32:36]
        share(me, pk_own.at[turn], pk_all.at[turn], share_sems[turn])
        pk_all[turn, me] = pk_own[turn]
        return total

    def key_side(turn):
        heads = [turn * TEAM + n for n in team]
        lams = [jnp.concatenate([lam_ref[2 * h], lam_ref[2 * h + 1]], axis=0) for h in heads]
        kus = [unit(zk_ref[h]) for h in heads]
        ws = [w_ref[h] for h in heads]
        dhops = [lead_last * mm(s_ref[h], lams[n], TN) for n, h in enumerate(heads)]
        drs = []
        for n, h in enumerate(heads):
            dwk = sc_ref[h, :, :HEAD] - d3(kus[n], dhops[n], NT)
            dwv = sc_ref[h, :, HEAD:] + tail * d2(kus[n], lams[n], NT)
            drs.append(d3(t_ref[h], jnp.concatenate([dwk, dwv], axis=1), TN))
        dkus = [
            qe_ref[h]
            - d3(ws[n][:, :HEAD], dhops[n], NN)
            + tail * d2(ws[n][:, HEAD:], lams[n], NN)
            for n, h in enumerate(heads)
        ]
        dlows = [jnp.where(strict, -d3(drs[n], ws[n], NT), 0.0) for n in team]
        kterms = [drs[n][:, :HEAD] + d3(dlows[n], kus[n], NN) for n in team]
        dkm_rows, extra = [], []
        for n, h in enumerate(heads):
            beta = beta_ref[h]
            dbeta = jnp.sum(kterms[n] * kus[n] + drs[n][:, HEAD:] * v, axis=-1, keepdims=True)
            dku = dkus[n] + beta * kterms[n] + d3(beta * dlows[n], kus[n], TN)
            dkm = d2r(k, unit_back(zk_ref[h], dku), TN)
            dlogit = dbeta * beta * (1.0 - beta)
            q = q_ref[:, lanes(h)].astype(f32)
            dkm_rows.append(dkm.reshape(SEQ, 8, HEAD))
            extra.append(jnp.sum(q * dlogit, axis=0, keepdims=True))
        extra = jnp.concatenate(extra + [loss, jnp.zeros((3, HEAD), f32)], axis=0)
        pk[turn, :, :32] = jnp.concatenate(dkm_rows, axis=1)
        pk[turn, :, 32:] = jnp.broadcast_to(extra[None], (SEQ, 8, HEAD))
        spread(me, pk.at[turn], pk_got.at[turn], key_sems[turn], [p for _, p in seq_peers(me)])

    key_side(0)
    pq_got[me] = pq[me]
    settle(me, pq, pq_got, (send3, recv3))
    pq_own[...] = lax.fori_loop(
        0, SEQ, lambda i, total: total + pq_got[i], jnp.zeros((half, HEAD), f32)
    ).astype(bf16)
    share(me, pq_own, pq_all, (send4, recv4))
    pq_all[me] = pq_own[...]
    key_side(1)
    key_total(0)
    total = key_total(1)
    loss_out[...] = total[36:37]
    settle_share(me, pq_own, pq_all, (send4, recv4))
    dq_ref[...] = pq_all[...]
    for turn in range(2):
        settle_share(me, pk_own.at[turn], pk_all.at[turn], share_sems[turn])
    dk_ref[...] = pk_all[...]


def finish_kernel(dq_in, dk_in, row_in, loss_in, dq_ref, dk_ref, row_ref, loss_ref):
    dq_ref[...] = dq_in[...].astype(f32)
    for turn in range(HEADS // TEAM):
        wide = dk_in[turn].astype(f32)
        for n in range(TEAM):
            dk_ref[turn * TEAM + n] = wide[:, n * 8 : (n + 1) * 8].reshape(HEAD, HEAD)
    row_ref[...] = row_in[...]
    loss_ref[...] = loss_in[:, :1] / (SEQ * ROWS * WIDTH)


def shape(dims, dtype):
    return jax.ShapeDtypeStruct(dims, dtype)


SMEM = pl.BlockSpec(memory_space=pltpu.SMEM)
VMEM = pl.BlockSpec(memory_space=pltpu.VMEM)
ANY = pl.BlockSpec(memory_space=pl.ANY)


def params(**more):
    return pltpu.CompilerParams(vmem_limit_bytes=VMEM_BYTES, has_side_effects=True, **more)


def shards(q, k, v, lens, proj, query_map, key_map, beta_weight, beta_bias):
    bw = beta_weight.reshape(HEADS, 1, HEAD)
    square = (HEADS, ROWS, ROWS)
    slab = (HEADS, ROWS, HEAD)
    halves = (SEQ, HEAD // 2, HEAD)
    extended = (2, SEQ, 40, HEAD)
    shares = (2, SEQ, 32, HEAD)
    block = (2, ROWS, HALF)
    scratch = [
        (slab, f32), (slab, f32), ((HEADS, ROWS, 1), f32), (square, f32), (square, f32),
        (square, f32), (slab, f32), ((ROWS, HEADS * HEAD), f32),
        ((1, HALF), f32), ((ROWS, HEADS * HEAD), bf16), ((HEADS, HEAD, HEAD), bf16),
        ((SEQ, HEAD, HEAD), bf16),
        ((SEQ, 192, HEAD), bf16), ((SEQ, 192, HEAD), bf16), (halves, bf16),
        ((4, 4, ROWS, HEAD), bf16), ((4, 4, ROWS, HEAD), bf16),
        (halves, bf16), (halves, bf16), (halves, bf16), (halves, bf16),
        (halves, f32), (halves, f32), (halves[1:], bf16), (halves, bf16),
        (extended, f32), (extended, f32), ((2, 32, HEAD), bf16), (shares, bf16),
        ((16, HEADS * HEAD, HALF), bf16), ((4,) + block, bf16), ((4,) + block, bf16),
        (block, bf16), (block, bf16), (block, bf16), (block[1:], bf16), (block[1:], bf16),
        (block, bf16), (block, bf16), ((8,) + block, bf16),
    ]
    sems = [16, 4, 4, 6, 6, 11, 11] + [SEQ] * 22
    partial = pl.pallas_call(
        whole_kernel,
        in_specs=[SMEM, SMEM] + [VMEM] * 6 + [ANY],
        out_specs=[VMEM] * 4,
        out_shape=[
            shape(halves, bf16), shape(shares, bf16), shape((HEADS, HEAD), f32),
            shape((1, HEAD), f32),
        ],
        scratch_shapes=[pltpu.VMEM(dims, kind) for dims, kind in scratch]
        + [pltpu.SemaphoreType.DMA((count,)) for count in sems],
        compiler_params=params(collective_id=0),
        name="whole",
    )(lens, beta_bias, q, k, v, query_map, key_map, bw, proj)
    grad_query, grad_key, grad_beta, loss = pl.pallas_call(
        finish_kernel,
        in_specs=[VMEM] * 4,
        out_specs=[VMEM] * 4,
        out_shape=[
            shape(halves, f32), shape((HEADS, HEAD, HEAD), f32), shape((HEADS, HEAD), f32),
            shape((1, 1), f32),
        ],
        name="finish",
    )(*partial)
    return loss.reshape(()), grad_query.reshape(HEADS, HEAD, HEAD), grad_key, grad_beta


def solution(mesh):
    return jax.shard_map(
        shards,
        mesh=mesh,
        in_specs=(
            P("seq", "head"),
            P("seq", "head"),
            P("seq", "head"),
            P(),
            P("head", None),
            P("head", None, None),
            P("head", None, None),
            P("head", None),
            P("head"),
        ),
        out_specs=(P(), P("head", None, None), P("head", None, None), P("head", None)),
        check_vma=False,
    )
```
